256 devices in a mesh: gx: 4 (over y), gy: 16 (over z_lo, x, core), gz: 4 (over z_hi).
Axes of the slice: x: 4, y: 4, z: 8 (z_hi: 4, z_lo: 2; z = z_hi * 2 + z_lo), core: 2. Of those that a mesh axis runs over, the one named last changes fastest.
Arguments:
- species: int32 [4, 16, 4, 128], P('gx', 'gy', 'gz'), may hold values from 0 to 4
- atom_count: int32 [4, 16, 4], P('gx', 'gy', 'gz'), may hold values from 64 to 128, as said below
- send_list: int32 [4, 16, 4, 32], P('gx', 'gy', 'gz'), may hold values from 0 to 127, as said below
- edge_count: int32 [4, 16, 4], P('gx', 'gy', 'gz'), may hold values from 512 to 2560, as said below
- edge_center: int32 [4, 16, 4, 2560], P('gx', 'gy', 'gz'), may hold values from 0 to 127, as said below
- edge_neighbour: int32 [4, 16, 4, 2560], P('gx', 'gy', 'gz'), may hold values from 0 to 991, as said below
- edge_vectors: float32 [4, 16, 4, 3, 2560], P('gx', 'gy', 'gz'), may hold values from -4.6 to 4.6, as said below
- embed: float32 [5, 128], replicated, may hold values from -6 to 6
- w_src: bfloat16 [2, 128, 192], replicated, may hold values from -0.5 to 0.5
- w_rad0: bfloat16 [2, 8, 64], replicated, may hold values from -2 to 2
- w_rad1: bfloat16 [2, 64, 256], replicated, may hold values from -0.75 to 0.75
- w_inv: bfloat16 [2, 64, 128], replicated, may hold values from -0.75 to 0.75
- w_out: bfloat16 [2, 128, 128], replicated, may hold values from -0.5 to 0.5
- w_gate: bfloat16 [2, 128, 64], replicated, may hold values from -0.5 to 0.5
- w_energy: float32 [128], replicated, may hold values from -0.5 to 0.5
Outputs:
- energies: float32 [4, 16, 4, 128], P('gx', 'gy', 'gz')
- forces: float32 [4, 16, 4, 3, 128], P('gx', 'gy', 'gz')
The draws below stay inside these ranges and needn't reach their ends.
Inputs may be any that keep to these rules, and one draw needn't show every extreme that they name: `atom_count`: domains of dense protein hold more live atoms; some domain is full. `edge_count`: dense domains hold more live edges than watery ones; some domain is full. `send_list`: every entry is a live atom of the domain. `edge_center`: live edges receive at live atoms; edges from the edge_count-th on are 0. `edge_neighbour`: A live edge sends from a live local atom or from a ghost row of another domain inside the slab (never the domain itself); edges from the edge_count-th on are 0. `edge_vectors`: every edge is between 0.9 and 4.6 long.
All inputs are finite; a program needn't handle non-finite values.
Results may differ from the reference program's by a relative error of at most 0.023.
Values may be sent and summed in bfloat16 or wider, within the bound.
A program may use at most 64 MiB of HBM per device.

```python
import math
import jax
import jax.numpy as jnp
from jax import lax

ATOMS_DEV = 128
SCALARS = 128
TENSORS = 64
RADIAL = 8
RADIAL_HID = 64
SPECIES = 5
LAYERS = 2
EDGES_DEV = 2560
SENDS_DEV = 32
N_GX = 4
N_GY = 16
N_GZ = 4


def draw_counts(key):
    devices = N_GX * N_GY * N_GZ
    key_dense, key_atoms, key_edges, key_full_a, key_full_e = jax.random.split(jax.random.fold_in(key, 101), 5)
    dense = jax.random.randint(key_dense, (devices,), 0, 4) == 0
    atom_low = jnp.where(dense, 3 * ATOMS_DEV // 4, ATOMS_DEV // 2)
    atom_high = jnp.where(dense, ATOMS_DEV + 1, 3 * ATOMS_DEV // 4 + 1)
    edge_low = jnp.where(dense, 3 * EDGES_DEV // 4, EDGES_DEV // 5)
    edge_high = jnp.where(dense, EDGES_DEV + 1, EDGES_DEV // 2 + 1)
    atom_counts = jax.random.randint(key_atoms, (devices,), atom_low, atom_high)
    edge_counts = jax.random.randint(key_edges, (devices,), edge_low, edge_high)
    atom_counts = atom_counts.at[jax.random.randint(key_full_a, (), 0, devices)].set(ATOMS_DEV)
    edge_counts = edge_counts.at[jax.random.randint(key_full_e, (), 0, devices)].set(EDGES_DEV)
    return (atom_counts, edge_counts)


def draw_edges(key):
    atom_counts, edge_counts = draw_counts(key)
    devices = N_GX * N_GY * N_GZ
    grid_shape = (devices, EDGES_DEV)
    keys = jax.random.split(jax.random.fold_in(key, 5), 7)
    live_slots = jnp.arange(EDGES_DEV)[None, :] < edge_counts[:, None]
    center = jnp.sort(jax.random.randint(keys[0], grid_shape, 0, atom_counts[:, None]), axis=1)
    local_ids = jax.random.randint(keys[1], grid_shape, 0, atom_counts[:, None])
    height = (jnp.arange(devices) % N_GZ)[:, None]
    step_x = jax.random.randint(keys[2], grid_shape, 0, 3)
    step_y = jax.random.randint(keys[3], grid_shape, 0, 3)
    step_z = jax.random.randint(keys[4], grid_shape, jnp.where(height == 0, 1, 0), jnp.where(height == N_GZ - 1, 2, 3))
    step_x = jnp.where((step_x == 1) & (step_y == 1) & (step_z == 1), 0, step_x)
    place_ids = jax.random.randint(keys[5], grid_shape, 0, SENDS_DEV)
    ghost_ids = ATOMS_DEV + ((step_x * 3 + step_y) * 3 + step_z) * SENDS_DEV + place_ids
    choose = jax.random.randint(keys[6], grid_shape, 0, 5) < 3
    neighbour = jnp.where(choose, local_ids, ghost_ids)
    center = jnp.where(live_slots, center, 0)
    neighbour = jnp.where(live_slots, neighbour, 0)
    return (center, neighbour)


def draw_atom_count(key, part):
    atom_counts, edge_counts = draw_counts(key)
    return atom_counts.reshape(N_GX, N_GY, N_GZ)


def draw_edge_count(key, part):
    atom_counts, edge_counts = draw_counts(key)
    return edge_counts.reshape(N_GX, N_GY, N_GZ)


def draw_send_list(key, part):
    atom_counts, edge_counts = draw_counts(key)
    key = jax.random.fold_in(key, 11)
    rows_drawn = jax.random.randint(key, (N_GX * N_GY * N_GZ, SENDS_DEV), 0, atom_counts[:, None])
    return rows_drawn.reshape(N_GX, N_GY, N_GZ, SENDS_DEV)


def draw_edge_center(key, part):
    center, neighbour = draw_edges(key)
    return center.reshape(N_GX, N_GY, N_GZ, EDGES_DEV)


def draw_edge_neighbour(key, part):
    center, neighbour = draw_edges(key)
    return neighbour.reshape(N_GX, N_GY, N_GZ, EDGES_DEV)


def draw_edge_vectors(key, part):
    key = jax.random.fold_in(key, 23)
    key_len, key_cos, key_azi = jax.random.split(key, 3)
    grid_shape = (N_GX, N_GY, N_GZ, EDGES_DEV)
    length = jax.random.uniform(key_len, grid_shape, jnp.float32, 0.9, 4.6)
    cosine = jax.random.uniform(key_cos, grid_shape, jnp.float32, -1.0, 1.0)
    azimuth = jax.random.uniform(key_azi, grid_shape, jnp.float32, -math.pi, math.pi)
    sine_part = jnp.sqrt(jnp.maximum(1.0 - cosine * cosine, 0.0))
    return jnp.stack([length * sine_part * jnp.cos(azimuth), length * sine_part * jnp.sin(azimuth), length * cosine], axis=3)


def set_ends(array, own_key, smallest, high):
    spot = [jax.random.randint(jax.random.fold_in(own_key, axis), (), 0, length) for axis, length in enumerate(array.shape)]
    widest = array.shape.index(max(array.shape))
    beside = spot[:widest] + [(spot[widest] + 1) % array.shape[widest]] + spot[widest + 1:]
    return array.at[tuple(spot)].set(smallest).at[tuple(beside)].set(high)


def noise(stream_key, dims, scale, limit, held_as=jnp.bfloat16):
    result = scale * jax.random.normal(stream_key, dims, jnp.float32)
    return jnp.clip(result, min=-limit, max=limit).astype(held_as)


def setup_inputs(seed: int = 0) -> dict:
    key_list = jax.random.split(jax.random.key(seed), 16)
    species = set_ends(jax.random.randint(key_list[0], (N_GX, N_GY, N_GZ, ATOMS_DEV), 0, SPECIES), jax.random.fold_in(key_list[0], 1), 0, SPECIES - 1).astype(jnp.int32)
    atom_count = draw_atom_count(jax.random.fold_in(key_list[15], 71), 0)
    send_list = draw_send_list(jax.random.fold_in(key_list[15], 71), 0)
    edge_count = draw_edge_count(jax.random.fold_in(key_list[15], 71), 0)
    edge_center = draw_edge_center(jax.random.fold_in(key_list[15], 71), 0)
    edge_neighbour = draw_edge_neighbour(jax.random.fold_in(key_list[15], 71), 0)
    edge_vectors = draw_edge_vectors(jax.random.fold_in(key_list[15], 71), 0)
    embed = noise(key_list[7], (SPECIES, SCALARS), 1.0, 6.0, jnp.float32)
    w_src = noise(key_list[8], (LAYERS, SCALARS, SCALARS + TENSORS), SCALARS ** -0.5, 0.5)
    w_rad0 = noise(key_list[9], (LAYERS, RADIAL, RADIAL_HID), RADIAL ** -0.5, 2.0)
    w_rad1 = noise(key_list[10], (LAYERS, RADIAL_HID, SCALARS + 2 * TENSORS), RADIAL_HID ** -0.5, 0.75)
    w_inv = noise(key_list[11], (LAYERS, TENSORS, SCALARS), TENSORS ** -0.5, 0.75)
    w_out = noise(key_list[12], (LAYERS, SCALARS, SCALARS), SCALARS ** -0.5, 0.5)
    w_gate = noise(key_list[13], (LAYERS, SCALARS, TENSORS), SCALARS ** -0.5, 0.5)
    w_energy = noise(key_list[14], (SCALARS,), SCALARS ** -0.5, 0.5, jnp.float32)
    return {"species": species, "atom_count": atom_count, "send_list": send_list, "edge_count": edge_count, "edge_center": edge_center, "edge_neighbour": edge_neighbour, "edge_vectors": edge_vectors, "embed": embed, "w_src": w_src, "w_rad0": w_rad0, "w_rad1": w_rad1, "w_inv": w_inv, "w_out": w_out, "w_gate": w_gate, "w_energy": w_energy}


CUTOFF = 5.0

def edge_geometry(vectors):
    distance = jnp.sqrt(lax.optimization_barrier(jnp.sum(vectors * vectors, axis=0)))
    unit_vectors = vectors / distance[None, :]
    along_x = unit_vectors[0]
    along_y = unit_vectors[1]
    along_z = unit_vectors[2]
    root_three = math.sqrt(3.0)
    harmonics = jnp.stack([along_x, along_y, along_z, root_three * along_x * along_y, root_three * along_y * along_z, 0.5 * (3.0 * along_z * along_z - 1.0), root_three * along_x * along_z, 0.5 * root_three * (along_x * along_x - along_y * along_y)], axis=0)
    frequency = jnp.arange(1, RADIAL + 1, dtype=jnp.float32)[:, None] * (math.pi / CUTOFF)
    radius_ratio = distance / CUTOFF
    envelope = (1.0 - radius_ratio * radius_ratio) ** 2
    basis_values = jnp.sin(frequency * distance[None, :]) * (envelope / distance)[None, :]
    return (harmonics, basis_values.astype(jnp.bfloat16))

def layer_step(scalars, tensors, table_p, table_t, vectors, centers, neighbours, edge_weight, w_rad0, w_rad1, w_inv, w_out, w_gate):
    atom_total = scalars.shape[0]
    edge_total = vectors.shape[1]
    scalar_width = scalars.shape[1]
    channels = w_gate.shape[1]
    harmonics, basis_values = edge_geometry(vectors)
    hidden = jax.nn.silu(lax.dot_general(basis_values, w_rad0, (((0,), (0,)), ((), ())), preferred_element_type=jnp.float32)).astype(jnp.bfloat16)
    radial = jnp.dot(hidden, w_rad1, preferred_element_type=jnp.float32)
    radial_s = radial[:, :scalar_width]
    radial_t = radial[:, scalar_width:scalar_width + channels]
    radial_u = radial[:, scalar_width + channels:]
    picked = table_p[neighbours]
    angular = harmonics.T[:, :, None]
    scalar_msg = picked[:, :scalar_width] * radial_s
    tensor_msg = (picked[:, scalar_width:] * radial_t)[:, None, :] * angular
    if table_t is not None:
        tensor_rows = table_t[neighbours].reshape(edge_total, 8, channels)
        invariant = lax.optimization_barrier(jnp.sum(tensor_rows * angular, axis=1)).astype(jnp.bfloat16)
        scalar_msg = scalar_msg + jnp.dot(invariant, w_inv, preferred_element_type=jnp.float32)
        tensor_msg = tensor_msg + tensor_rows * radial_u[:, None, :]
    gathered_s = jax.ops.segment_sum(scalar_msg * edge_weight[:, None], centers, num_segments=atom_total)
    gathered_t = jax.ops.segment_sum(tensor_msg.reshape(edge_total, 8 * channels) * edge_weight[:, None], centers, num_segments=atom_total)
    rounded = gathered_s.astype(jnp.bfloat16)
    new_s = scalars + jax.nn.silu(jnp.dot(rounded, w_out, preferred_element_type=jnp.float32))
    gate_values = jax.nn.sigmoid(jnp.dot(rounded, w_gate, preferred_element_type=jnp.float32))
    new_t = (gathered_t.reshape(atom_total, 8, channels) * gate_values[:, None, :]).reshape(atom_total, 8 * channels)
    if tensors is not None:
        new_t = new_t + tensors
    return (new_s, new_t)

def reference(species, atom_count, send_list, edge_count, edge_center, edge_neighbour, edge_vectors, embed, w_src, w_rad0, w_rad1, w_inv, w_out, w_gate, w_energy):
    devices = N_GX * N_GY * N_GZ
    atom_total = ATOMS_DEV
    send_total = SENDS_DEV
    edge_total = EDGES_DEV
    kind_ids = species.reshape(devices, atom_total)
    send_rows = send_list.reshape(devices, send_total)
    centers = edge_center.reshape(devices, edge_total)
    neighbours = edge_neighbour.reshape(devices, edge_total)
    vectors = edge_vectors.reshape(devices, 3, edge_total)
    atom_mask = (jnp.arange(atom_total)[None, :] < atom_count.reshape(devices)[:, None]).astype(jnp.float32)
    edge_weight = 0.25 * (jnp.arange(edge_total)[None, :] < edge_count.reshape(devices)[:, None]).astype(jnp.float32)
    device = jnp.arange(devices)
    pos_x = device // (N_GY * N_GZ)
    pos_y = device // N_GZ % N_GY
    pos_z = device % N_GZ
    slot_ids = jnp.arange(27)
    source_x = (pos_x[:, None] + slot_ids[None, :] // 9 - 1) % N_GX
    source_y = (pos_y[:, None] + slot_ids[None, :] // 3 % 3 - 1) % N_GY
    source_z = pos_z[:, None] + slot_ids[None, :] % 3 - 1
    inside = ((source_z >= 0) & (source_z < N_GZ)).astype(jnp.float32)
    source = (source_x * N_GY + source_y) * N_GZ + jnp.clip(source_z, 0, N_GZ - 1)
    onehot = jax.nn.one_hot(kind_ids.reshape(-1), SPECIES, dtype=jnp.float32)
    start_rows = jnp.dot(onehot, embed, precision=lax.Precision.HIGHEST).astype(jnp.bfloat16).reshape(devices, atom_total, SCALARS)

    def project(scalars, layer):
        flat_rows = scalars.reshape(devices * atom_total, SCALARS)
        return jnp.dot(flat_rows, w_src[layer], preferred_element_type=jnp.float32).astype(jnp.bfloat16).reshape(devices, atom_total, SCALARS + TENSORS)

    def lend(rows):
        return jnp.take_along_axis(rows, send_rows[:, :, None], axis=1).astype(jnp.float32)

    def ghost_of(buffer, index):
        scale = inside[index][:, None, None]
        return (buffer[source[index]] * scale).astype(jnp.bfloat16).reshape(27 * send_total, buffer.shape[2])

    def energy_sum(moved_all):
        proj_start = project(start_rows, 0)
        lent_start = lend(proj_start)

        def first(inputs):
            index, moved = inputs
            table_p = jnp.concatenate([proj_start[index], ghost_of(lent_start, index)], axis=0)
            new_s, new_t = layer_step(start_rows[index], None, table_p, None, moved, centers[index], neighbours[index], edge_weight[index], w_rad0[0], w_rad1[0], w_inv[0], w_out[0], w_gate[0])
            return (new_s.astype(jnp.bfloat16), new_t.astype(jnp.bfloat16))
        scalars_one, tensors_one = lax.map(jax.checkpoint(first), (device, moved_all))
        proj_one = project(scalars_one, 1)
        lent_p = lend(proj_one)
        lent_t = lend(tensors_one)

        def second(inputs):
            index, moved = inputs
            table_p = jnp.concatenate([proj_one[index], ghost_of(lent_p, index)], axis=0)
            table_t = jnp.concatenate([tensors_one[index], ghost_of(lent_t, index)], axis=0)
            new_s, new_t = layer_step(scalars_one[index], tensors_one[index], table_p, table_t, moved, centers[index], neighbours[index], edge_weight[index], w_rad0[1], w_rad1[1], w_inv[1], w_out[1], w_gate[1])
            return atom_mask[index] * lax.optimization_barrier(jnp.sum(new_s * w_energy[None, :], axis=1))
        energies = lax.map(jax.checkpoint(second), (device, moved_all))
        return (jnp.sum(energies), energies)
    grads, energies = jax.grad(energy_sum, has_aux=True)(vectors)
    is_local = neighbours < atom_total
    ghost_ids = jnp.clip(neighbours - atom_total, 0, 27 * send_total - 1)
    owner = jnp.take_along_axis(source, ghost_ids // send_total, axis=1)
    owner_row = send_rows[owner, ghost_ids % send_total]
    target_send = jnp.where(is_local, device[:, None] * atom_total + neighbours, owner * atom_total + owner_row)
    target_take = device[:, None] * atom_total + centers
    pull_rows = jnp.transpose(grads, (0, 2, 1)).reshape(devices * edge_total, 3)
    forces = jnp.zeros((devices * atom_total, 3), jnp.float32)
    forces = forces.at[target_take.reshape(-1)].add(pull_rows)
    forces = forces.at[target_send.reshape(-1)].add(-pull_rows)
    forces = forces.reshape(N_GX, N_GY, N_GZ, atom_total, 3).transpose(0, 1, 2, 4, 3)
    return (energies.reshape(N_GX, N_GY, N_GZ, atom_total), forces)
```

```python
import functools
import math

import jax
import jax.numpy as jnp
from jax import lax
from jax.experimental import pallas as pl
from jax.experimental.pallas import tpu as pltpu
from jax.sharding import PartitionSpec as P

RADIAL = 8
CUTOFF = 5.0
TILE = 256
MESH = pl.DeviceIdType.MESH
BF16 = jnp.bfloat16
F32 = jnp.float32


def mm(left, right):
    return lax.dot_general(left, right, (((1,), (0,)), ((), ())), preferred_element_type=F32)


def mm_nt(left, right):
    return lax.dot_general(left, right, (((1,), (1,)), ((), ())), preferred_element_type=F32)


def eye(rows, cols):
    first = lax.broadcasted_iota(jnp.int32, (rows, cols), 0)
    second = lax.broadcasted_iota(jnp.int32, (rows, cols), 1)
    return jnp.where(first == second, 1.0, 0.0).astype(BF16)


def turned(array):
    return mm_nt(eye(array.shape[1], array.shape[1]), array).astype(BF16)


def split(array):
    high = array.astype(BF16).astype(F32)
    return jnp.concatenate([high, array - high], axis=0).astype(BF16)


def joined(array):
    half = array.shape[0] // 2
    return array[:half] + array[half:]


def sum_rows(array):
    return jnp.sum(array, axis=0, keepdims=True)


def sin_cos(angle):
    y = angle - (math.pi / 2)
    y2 = y * y
    sin_y = jnp.full_like(y, -1.0 / math.factorial(11))
    for power in (9, 7, 5, 3, 1):
        sin_y = sin_y * y2 + ((-1.0) ** (power // 2)) / math.factorial(power)
    cos_y = jnp.full_like(y, 1.0 / math.factorial(12))
    for power in (10, 8, 6, 4, 2, 0):
        cos_y = cos_y * y2 + ((-1.0) ** (power // 2)) / math.factorial(power)
    return cos_y, -(sin_y * y)


def body(
    atom_count, edge_count, species, send_list, center, neighbour, vectors,
    embed, w_src, w_rad0, w_rad1, w_inv, w_out, w_gate, w_energy,
    energies, forces,
    onehot, onehot_c, kinds, halo, table, picked, dmsg,
    geo, harm, dbas, basis, slope, rad1, rad2, proj1, lead, agg, agg2, grad_y, grad_d, pull,
    back_send_y, back_recv_y, back_send_x, back_recv_x, back_send_z, back_recv_z,
    f_send_y, f_recv_y, f_send_x, f_recv_x, f_send_z, f_recv_z,
    send_sems, recv_sems,
):
    atoms = species.shape[1]
    edges = center.shape[1]
    sends = send_list.shape[1]
    width = w_out.shape[1]
    chan = w_gate.shape[2]
    rows_x = 3 * sends
    rows_y = 9 * sends
    ghosts = 27 * sends
    tiles = edges // TILE
    own_row = (9 + 3 + 1) * sends

    def step(axis, by):
        size = lax.axis_size(axis)
        return {axis: lax.rem(lax.axis_index(axis) + size + by, size)}

    barrier = pltpu.get_barrier_semaphore()
    for axis in ("gx", "gy", "gz"):
        for by in (1, -1):
            pl.semaphore_signal(barrier, inc=1, device_id=step(axis, by), device_id_type=MESH)

    next_sem = [0]
    started = []

    def send(source, target, axis, by):
        slot = next_sem[0]
        next_sem[0] = slot + 1
        copy = pltpu.make_async_remote_copy(
            src_ref=source, dst_ref=target, send_sem=send_sems.at[slot], recv_sem=recv_sems.at[slot],
            device_id=step(axis, by), device_id_type=MESH,
        )
        copy.start()
        started.append(copy)
        return copy

    def spread_start(ref):
        low = (9 + 3) * sends
        own = ref.at[pl.ds(own_row, sends)]
        return [
            send(own, ref.at[pl.ds(low, sends)], "gz", 1),
            send(own, ref.at[pl.ds(low + 2 * sends, sends)], "gz", -1),
        ]

    def spread_finish(ref, first):
        for copy in first:
            copy.wait_recv()
        middle = ref.at[pl.ds(rows_y + rows_x, rows_x)]
        along_x = [
            send(middle, ref.at[pl.ds(rows_y, rows_x)], "gx", 1),
            send(middle, ref.at[pl.ds(rows_y + 2 * rows_x, rows_x)], "gx", -1),
        ]
        last = []
        for part in (1, 0, 2):
            if part != 1:
                along_x[part // 2].wait_recv()
            rows = ref.at[pl.ds(rows_y + part * rows_x, rows_x)]
            last.append(send(rows, ref.at[pl.ds(part * rows_x, rows_x)], "gy", 1))
            last.append(send(rows, ref.at[pl.ds(2 * rows_y + part * rows_x, rows_x)], "gy", -1))
        for copy in last:
            copy.wait_recv()

    lane = lax.broadcasted_iota(jnp.int32, (atoms, atoms), 0)
    kind_t = jnp.where(lane == species[...], 1.0, 0.0).astype(BF16)
    lend_t = jnp.where(
        lax.broadcasted_iota(jnp.int32, (atoms, sends), 0) == send_list[...], 1.0, 0.0
    ).astype(BF16)
    lend = mm_nt(eye(sends, sends), lend_t).astype(BF16)
    kinds[pl.ds(own_row, sends), :] = mm_nt(lend, kind_t).astype(BF16)
    pl.semaphore_wait(barrier, 6)
    kinds_first = spread_start(kinds)

    live = lax.broadcasted_iota(jnp.int32, (1, edges), 1) < edge_count[0, 0]
    x = jnp.where(live, vectors[0:1, :], 1.0)
    y = jnp.where(live, vectors[1:2, :], 1.0)
    z = jnp.where(live, vectors[2:3, :], 1.0)
    square = x * x + y * y + z * z
    inverse = lax.rsqrt(square)
    distance = square * inverse
    ux, uy, uz = x * inverse, y * inverse, z * inverse
    root = math.sqrt(3.0)
    for row, value in enumerate((ux, uy, uz, inverse)):
        geo[pl.ds(row, 1), :] = value
    for row, value in enumerate((
        ux, uy, uz, root * ux * uy, root * uy * uz, 0.5 * (3.0 * uz * uz - 1.0), root * ux * uz,
        0.5 * root * (ux * ux - uy * uy),
    )):
        harm[pl.ds(row, 1), :] = value
    sine, cosine = sin_cos(distance * (math.pi / CUTOFF))
    ratio = distance * (1.0 / CUTOFF)
    rest = 1.0 - ratio * ratio
    scale = rest * rest * inverse
    dscale = -(4.0 / CUTOFF) * rest * ratio * inverse - scale * inverse
    sin_k, cos_k = sine, cosine
    basis[...] = jnp.zeros_like(basis)
    for k in range(1, RADIAL + 1):
        basis[pl.ds(k - 1, 1), :] = sin_k * scale
        dbas[pl.ds(k - 1, 1), :] = (k * math.pi / CUTOFF) * cos_k * scale + sin_k * dscale
        sin_k, cos_k = sin_k * cosine + cos_k * sine, cos_k * cosine - sin_k * sine

    near = neighbour[...]
    ghost = near - atoms
    part_a = jnp.where(ghost >= rows_y, 1, 0) + jnp.where(ghost >= 2 * rows_y, 1, 0)
    ghost = ghost - rows_y * part_a
    part_b = jnp.where(ghost >= rows_x, 1, 0) + jnp.where(ghost >= 2 * rows_x, 1, 0)
    ghost = ghost - rows_x * part_b + rows_x * part_a + rows_y * part_b + atoms
    place = jnp.where(live, jnp.where(near < atoms, near, ghost), -1)
    middle_atom = jnp.where(live, center[...], -1)
    lead[pl.ds(0, 1), :] = place
    lead[pl.ds(1, 1), :] = middle_atom

    src1_t = turned(w_src[0])
    src2_t = turned(w_src[1])
    rad0_t = jnp.concatenate(
        [
            turned(jnp.concatenate([w_rad0[l].astype(F32), jnp.zeros((8, w_rad0.shape[2]), F32)], axis=0).astype(BF16))
            .astype(F32)
            for l in range(2)
        ],
        axis=0,
    ).astype(BF16)
    hid = w_rad0.shape[2]
    rad1_t1 = turned(w_rad1[0][:, : width + chan])
    rad1_t2 = turned(w_rad1[1][:, :width])
    inv_t = turned(w_inv[1])
    out1_t = turned(w_out[0])
    out2_t = turned(w_out[1])
    gate_t = turned(w_gate[0])
    embed_rows = jnp.concatenate([embed[...], jnp.zeros((16 - embed.shape[0], width), F32)], axis=0)
    embed_t = turned(embed_rows.astype(BF16))
    kind_proj = mm(src1_t, embed_t).astype(BF16)
    start = mm(embed_t, kind_t[:16, :])

    def cut(i):
        return pl.ds(pl.multiple_of(i * TILE, TILE), TILE)

    def prepare(i, carry):
        span = cut(i)
        rows = lax.broadcasted_iota(jnp.int32, (onehot.shape[0], TILE), 0)
        onehot[:, span] = jnp.where(rows == lead[0:1, span], 1.0, 0.0).astype(BF16)
        rows = lax.broadcasted_iota(jnp.int32, (atoms, TILE), 0)
        onehot_c[:, span] = jnp.where(rows == lead[1:2, span], 1.0, 0.0).astype(BF16)
        pre = mm(rad0_t, basis[:, span].astype(BF16))
        sig = jax.nn.sigmoid(pre)
        slope[:, span] = sig * (1.0 + pre * (1.0 - sig))
        hidden = (pre * sig).astype(BF16)
        rad1[:, span] = mm(rad1_t1, hidden[:hid])
        rad2[:, span] = mm(rad1_t2, hidden[hid:])
        return carry

    lax.fori_loop(0, tiles, prepare, 0)

    spread_finish(kinds, kinds_first)
    ghost_kinds = mm_nt(eye(16, kinds.shape[1]), kinds[...]).astype(BF16)
    agg[...] = jnp.zeros_like(agg)

    def layer_one(i, carry):
        span = cut(i)
        kind = mm(kind_t[:16], onehot[pl.ds(0, atoms), span]) + mm(
            ghost_kinds, onehot[pl.ds(atoms, ghosts), span]
        )
        proj = mm(kind_proj, kind.astype(BF16))
        proj1[:, span] = proj
        lead_s = proj[:width] * rad1[pl.ds(0, width), span]
        lead_t = proj[width:] * rad1[pl.ds(width, chan), span]
        parts = [lead_s.astype(BF16)]
        for m in range(8):
            parts.append((lead_t * harm[pl.ds(m, 1), span]).astype(BF16))
        agg[...] += mm_nt(jnp.concatenate(parts, axis=0), onehot_c[:, span])
        return carry

    lax.fori_loop(0, tiles, layer_one, 0)
    gathered = 0.25 * agg[...]
    gathered_t = gathered[width:]
    rounded = gathered[:width].astype(BF16)
    pre1 = mm(out1_t, rounded)
    sig1 = jax.nn.sigmoid(pre1)
    gate = jax.nn.sigmoid(mm(gate_t, rounded))
    scalars = (start + pre1 * sig1).astype(BF16)
    gates = jnp.concatenate([gate] * 8, axis=0)
    tensors = (gathered_t * gates).astype(BF16)
    proj2 = mm(src2_t, scalars).astype(BF16)
    local = jnp.concatenate([proj2[:width], tensors], axis=0)
    halo[pl.ds(own_row, sends), :] = mm_nt(lend, local).astype(BF16)
    halo_first = spread_start(halo)
    table[:, pl.ds(0, atoms)] = local
    spread_finish(halo, halo_first)
    table[:, pl.ds(atoms, ghosts)] = halo[...].T
    agg2[...] = jnp.zeros_like(agg2)

    def layer_two(i, carry):
        span = cut(i)
        rows = mm(table[...], onehot[pl.ds(0, atoms + ghosts), span])
        picked[:, span] = rows.astype(BF16)
        inner = jnp.zeros((chan, TILE), F32)
        for m in range(8):
            inner += rows[width + m * chan : width + (m + 1) * chan] * harm[pl.ds(m, 1), span]
        message = rows[:width] * rad2[:, span] + mm(inv_t, inner.astype(BF16))
        agg2[...] += mm_nt(message.astype(BF16), onehot_c[:, span])
        return carry

    lax.fori_loop(0, tiles, layer_two, 0)
    rounded = (0.25 * agg2[...]).astype(BF16)
    pre2 = mm(out2_t, rounded)
    sig2 = jax.nn.sigmoid(pre2)
    readout = jnp.broadcast_to(w_energy[...], (width, width)).T[:, :1]
    mask = jnp.where(
        lax.broadcasted_iota(jnp.int32, (1, atoms), 1) < atom_count[0, 0], 1.0, 0.0
    )
    energies[...] = mask * sum_rows((scalars.astype(F32) + pre2 * sig2) * readout)

    d_new = readout * mask
    d_pre = (d_new * sig2 * (1.0 + pre2 * (1.0 - sig2))).astype(BF16)
    d_agg = (0.25 * mm(w_out[1], d_pre).astype(BF16).astype(F32)).astype(BF16)

    def back_two(i, carry):
        span = cut(i)
        d_msg = mm(d_agg, onehot_c[:, span])
        dmsg[pl.ds(0, width), span] = (d_msg * rad2[:, span]).astype(BF16)
        d_inv = mm(w_inv[1], d_msg.astype(BF16))
        for m in range(8):
            dmsg[pl.ds(width + m * chan, chan), span] = (d_inv * harm[pl.ds(m, 1), span]).astype(BF16)
        return carry

    lax.fori_loop(0, tiles, back_two, 0)
    back_y = []
    for slot, part, by in ((0, 0, -1), (1, 2, 1)):
        back_send_y[slot] = mm_nt(
            onehot[pl.ds(atoms + part * rows_y, rows_y), :], dmsg[...]
        ).astype(BF16)
        back_y.append(send(back_send_y.at[slot], back_recv_y.at[slot], "gy", by))
    back = mm_nt(onehot[pl.ds(atoms + rows_y, rows_y), :], dmsg[...])
    d_local = mm_nt(dmsg[...], onehot[pl.ds(0, atoms), :])

    def edge_two(i, carry):
        span = cut(i)
        d_msg = mm(d_agg, onehot_c[:, span])
        d_inv = mm(w_inv[1], d_msg.astype(BF16))
        for m in range(8):
            grad_y[pl.ds(m, 1), span] = sum_rows(
                d_inv * picked[pl.ds(width + m * chan, chan), span].astype(F32)
            )
        d_rad = (d_msg * picked[pl.ds(0, width), span].astype(F32)).astype(BF16)
        d_hid = mm(w_rad1[1][:, :width], d_rad) * slope[pl.ds(hid, hid), span]
        d_bas = mm(w_rad0[1], d_hid.astype(BF16))
        grad_d[:, span] = sum_rows(d_bas * dbas[:, span])
        return carry

    lax.fori_loop(0, tiles, edge_two, 0)
    for copy in back_y:
        copy.wait_recv()
    back = back + back_recv_y[0].astype(F32) + back_recv_y[1].astype(F32)
    back_x = []
    for slot, part, by in ((0, 0, -1), (1, 2, 1)):
        back_send_x[slot] = back[part * rows_x : (part + 1) * rows_x].astype(BF16)
        back_x.append(send(back_send_x.at[slot], back_recv_x.at[slot], "gx", by))
    back = back[rows_x : 2 * rows_x]
    for copy in back_x:
        copy.wait_recv()
    back = back + back_recv_x[0].astype(F32) + back_recv_x[1].astype(F32)
    back_z = []
    for slot, part, by in ((0, 0, -1), (1, 2, 1)):
        back_send_z[slot] = back[part * sends : (part + 1) * sends].astype(BF16)
        back_z.append(send(back_send_z.at[slot], back_recv_z.at[slot], "gz", by))
    back = back[sends : 2 * sends]
    for copy in back_z:
        copy.wait_recv()
    back = back + back_recv_z[0].astype(F32) + back_recv_z[1].astype(F32)
    owned = d_local + mm(back.T.astype(BF16), lend)

    d_scalars = (d_new + mm(w_src[1][:, :width], owned[:width].astype(BF16))).astype(BF16).astype(F32)
    d_tensors = owned[width:].astype(BF16).astype(F32)
    d_pre = (d_scalars * sig1 * (1.0 + pre1 * (1.0 - sig1))).astype(BF16)
    product = d_tensors * gathered_t
    d_gate = jnp.zeros((chan, atoms), F32)
    for m in range(8):
        d_gate += product[m * chan : (m + 1) * chan]
    d_gate = (d_gate * gate * (1.0 - gate)).astype(BF16)
    d_scalar_agg = (mm(w_out[0], d_pre) + mm(w_gate[0], d_gate)).astype(BF16).astype(F32)
    d_agg1 = (0.25 * jnp.concatenate([d_scalar_agg, d_tensors * gates], axis=0)).astype(BF16)

    def edge_one(i, carry):
        span = cut(i)
        d_msg = mm(d_agg1, onehot_c[:, span])
        proj = proj1[:, span]
        lead_t = proj[width:] * rad1[pl.ds(width, chan), span]
        inner = jnp.zeros((chan, TILE), F32)
        gy = []
        for m in range(8):
            d_part = d_msg[width + m * chan : width + (m + 1) * chan]
            inner += d_part * harm[pl.ds(m, 1), span]
            gy.append(grad_y[pl.ds(m, 1), span] + sum_rows(d_part * lead_t))
        d_rad = jnp.concatenate([d_msg[:width], inner], axis=0) * proj
        d_hid = mm(w_rad1[0][:, : width + chan], d_rad.astype(BF16)) * slope[pl.ds(0, hid), span]
        d_bas = mm(w_rad0[0], d_hid.astype(BF16))
        gd = grad_d[:, span] + sum_rows(d_bas * dbas[:, span])
        ax, ay, az = geo[0:1, span], geo[1:2, span], geo[2:3, span]
        gux = gy[0] + root * (ay * gy[3] + az * gy[6] + ax * gy[7])
        guy = gy[1] + root * (ax * gy[3] + az * gy[4] - ay * gy[7])
        guz = gy[2] + root * (ay * gy[4] + ax * gy[6]) + 3.0 * az * gy[5]
        radial = gd - geo[3:4, span] * (ax * gux + ay * guy + az * guz)
        pull[pl.ds(0, 1), span] = geo[3:4, span] * gux + ax * radial
        pull[pl.ds(1, 1), span] = geo[3:4, span] * guy + ay * radial
        pull[pl.ds(2, 1), span] = geo[3:4, span] * guz + az * radial
        return carry

    pull[...] = jnp.zeros_like(pull)
    lax.fori_loop(0, tiles, edge_one, 0)

    halves = split(pull[...])

    def slab(part_b, part_a):
        first = atoms + part_b * rows_y + part_a * rows_x
        return joined(mm_nt(halves, onehot[pl.ds(first, 128), :]))

    f_y = []
    for slot, part, by in ((0, 0, -1), (1, 2, 1)):
        for a in range(3):
            f_send_y[slot, :, pl.ds(a * 128, 128)] = slab(part, a)
        f_y.append(send(f_send_y.at[slot], f_recv_y.at[slot], "gy", by))
    total = joined(mm_nt(halves, onehot_c[...])) - joined(mm_nt(halves, onehot[pl.ds(0, atoms), :]))
    sums = [slab(1, a) for a in range(3)]
    for copy in f_y:
        copy.wait_recv()
    sums = [
        sums[a] + f_recv_y[0, :, pl.ds(a * 128, 128)] + f_recv_y[1, :, pl.ds(a * 128, 128)] for a in range(3)
    ]
    f_x = []
    for slot, part, by in ((0, 0, -1), (1, 2, 1)):
        f_send_x[slot] = sums[part]
        f_x.append(send(f_send_x.at[slot], f_recv_x.at[slot], "gx", by))
    for copy in f_x:
        copy.wait_recv()
    plane = sums[1] + f_recv_x[0] + f_recv_x[1]
    f_send_z[...] = plane
    f_z = [
        send(f_send_z, f_recv_z.at[0], "gz", -1),
        send(f_send_z, f_recv_z.at[1], "gz", 1),
    ]
    for copy in f_z:
        copy.wait_recv()
    plane = (
        pltpu.roll(plane, 128 - sends, 1) + f_recv_z[0] + pltpu.roll(f_recv_z[1], 128 - 2 * sends, 1)
    )
    lend_wide = mm_nt(eye(128, sends), lend_t).astype(BF16)
    total = total - joined(mm(split(plane), lend_wide))
    forces[...] = total[:3]
    for copy in started:
        copy.wait_send()


def per_device(
    species, atom_count, send_list, edge_count, edge_center, edge_neighbour, edge_vectors,
    embed, w_src, w_rad0, w_rad1, w_inv, w_out, w_gate, w_energy,
):
    atoms = species.shape[-1]
    edges = edge_center.shape[-1]
    sends = send_list.shape[-1]
    width = w_out.shape[1]
    chan = w_gate.shape[2]
    hid = w_rad0.shape[2]
    cols = width + 8 * chan
    ghosts = 27 * sends
    vmem = pl.BlockSpec(memory_space=pltpu.VMEM)
    smem = pl.BlockSpec(memory_space=pltpu.SMEM)
    copies = 10 + 10 + 6 + 6
    energies, forces = pl.pallas_call(
        body,
        out_shape=(
            jax.ShapeDtypeStruct((1, atoms), F32),
            jax.ShapeDtypeStruct((3, atoms), F32),
        ),
        in_specs=[smem, smem] + [vmem] * 13,
        out_specs=(vmem, vmem),
        scratch_shapes=[
            pltpu.VMEM((1024, edges), BF16),
            pltpu.VMEM((atoms, edges), BF16),
            pltpu.VMEM((ghosts, 128), BF16),
            pltpu.VMEM((ghosts, cols), BF16),
            pltpu.VMEM((cols, atoms + ghosts), BF16),
            pltpu.VMEM((cols, edges), BF16),
            pltpu.VMEM((cols, edges), BF16),
            pltpu.VMEM((8, edges), F32),
            pltpu.VMEM((8, edges), F32),
            pltpu.VMEM((8, edges), F32),
            pltpu.VMEM((16, edges), F32),
            pltpu.VMEM((2 * hid, edges), F32),
            pltpu.VMEM((width + chan, edges), F32),
            pltpu.VMEM((width, edges), F32),
            pltpu.VMEM((width + chan, edges), F32),
            pltpu.VMEM((8, edges), jnp.int32),
            pltpu.VMEM((cols, atoms), F32),
            pltpu.VMEM((width, atoms), F32),
            pltpu.VMEM((8, edges), F32),
            pltpu.VMEM((1, edges), F32),
            pltpu.VMEM((8, edges), F32),
            pltpu.VMEM((2, 9 * sends, cols), BF16),
            pltpu.VMEM((2, 9 * sends, cols), BF16),
            pltpu.VMEM((2, 3 * sends, cols), BF16),
            pltpu.VMEM((2, 3 * sends, cols), BF16),
            pltpu.VMEM((2, sends, cols), BF16),
            pltpu.VMEM((2, sends, cols), BF16),
            pltpu.VMEM((2, 8, 384), F32),
            pltpu.VMEM((2, 8, 384), F32),
            pltpu.VMEM((2, 8, 128), F32),
            pltpu.VMEM((2, 8, 128), F32),
            pltpu.VMEM((8, 128), F32),
            pltpu.VMEM((2, 8, 128), F32),
            pltpu.SemaphoreType.DMA((copies,)),
            pltpu.SemaphoreType.DMA((copies,)),
        ],
        compiler_params=pltpu.CompilerParams(
            collective_id=0, has_side_effects=True, vmem_limit_bytes=52 * 1024 * 1024
        ),
    )(
        atom_count.reshape(1, 1), edge_count.reshape(1, 1), species.reshape(1, atoms),
        send_list.reshape(1, sends), edge_center.reshape(1, edges), edge_neighbour.reshape(1, edges),
        edge_vectors.reshape(3, edges), embed, w_src, w_rad0, w_rad1, w_inv, w_out, w_gate,
        w_energy.reshape(1, width),
    )
    return energies.reshape(species.shape), forces.reshape(edge_vectors.shape[:3] + (3, atoms))


def solution(mesh):
    shard = P("gx", "gy", "gz", None)
    count = P("gx", "gy", "gz")
    wide = P("gx", "gy", "gz", None, None)
    return jax.shard_map(
        per_device,
        mesh=mesh,
        in_specs=(shard, count, shard, count, shard, shard, wide) + (P(),) * 8,
        out_specs=(shard, wide),
        check_vma=False,
    )
```

```python
import functools
import math

import jax
import jax.numpy as jnp
from jax import lax
from jax.experimental import pallas as pl
from jax.experimental.pallas import tpu as pltpu
from jax.sharding import PartitionSpec as P

RADIAL = 8
CUTOFF = 5.0
TILE = 1280
MESH = pl.DeviceIdType.MESH
BF16 = jnp.bfloat16
F32 = jnp.float32


def mm(left, right):
    return lax.dot_general(left, right, (((1,), (0,)), ((), ())), preferred_element_type=F32)


def mm_nt(left, right):
    return lax.dot_general(left, right, (((1,), (1,)), ((), ())), preferred_element_type=F32)


def eye(rows, cols):
    first = lax.broadcasted_iota(jnp.int32, (rows, cols), 0)
    second = lax.broadcasted_iota(jnp.int32, (rows, cols), 1)
    return jnp.where(first == second, 1.0, 0.0).astype(BF16)


def turned(array):
    return mm_nt(eye(array.shape[1], array.shape[1]), array).astype(BF16)


def split(array):
    high = array.astype(BF16).astype(F32)
    return jnp.concatenate([high, array - high], axis=0).astype(BF16)


def joined(array):
    half = array.shape[0] // 2
    return array[:half] + array[half:]


def sum_rows(array):
    return jnp.sum(array, axis=0, keepdims=True)


def sin_cos(angle):
    y = angle - (math.pi / 2)
    y2 = y * y
    sin_y = jnp.full_like(y, -1.0 / math.factorial(11))
    for power in (9, 7, 5, 3, 1):
        sin_y = sin_y * y2 + ((-1.0) ** (power // 2)) / math.factorial(power)
    cos_y = jnp.full_like(y, 1.0 / math.factorial(12))
    for power in (10, 8, 6, 4, 2, 0):
        cos_y = cos_y * y2 + ((-1.0) ** (power // 2)) / math.factorial(power)
    return cos_y, -(sin_y * y)


def body(
    atom_count, edge_count, *refs
):
    args, (energies, forces), held = refs[:13], refs[13:15], refs[15:28]
    (
        onehot, onehot_c, block_of, slot_of, kinds, halo, table, picked, dmsg,
        geo, harm, dbas, basis, slope, rad1, rad2, proj1, agg, agg2, grad_y, grad_d, pull,
        back_send_y, back_recv_y, back_send_x, back_recv_x, back_send_z, back_recv_z,
        f_all, f_recv_y, f_send_x, f_recv_x, f_send_z, f_recv_z,
        send_sems, recv_sems, arg_sems,
    ) = refs[28:]
    (
        species, send_list, vectors, neighbour, center,
        embed, w_src, w_rad0, w_rad1, w_inv, w_out, w_gate, w_energy,
    ) = held
    atoms = species.shape[1]
    edges = center.shape[1]
    sends = send_list.shape[1]
    width = w_out.shape[1]
    chan = w_gate.shape[1]
    rows_x = 3 * sends
    rows_y = 9 * sends
    ghosts = 27 * sends
    tiles = edges // TILE
    unit = 8
    blocks = atoms // sends + 27

    def step(axis, by):
        size = lax.axis_size(axis)
        return {axis: lax.rem(lax.axis_index(axis) + size + by, size)}

    barrier = pltpu.get_barrier_semaphore()
    for axis in ("gx", "gy", "gz"):
        for by in (1, -1):
            pl.semaphore_signal(barrier, inc=1, device_id=step(axis, by), device_id_type=MESH)

    loads = [
        pltpu.make_async_copy(source, target, arg_sems.at[i])
        for i, (source, target) in enumerate(zip(args, held))
    ]
    for load in loads:
        load.start()

    next_sem = [0]
    started = []

    def send(source, target, axis, by):
        slot = next_sem[0]
        next_sem[0] = slot + 1
        copy = pltpu.make_async_remote_copy(
            src_ref=source, dst_ref=target, send_sem=send_sems.at[slot], recv_sem=recv_sems.at[slot],
            device_id=step(axis, by), device_id_type=MESH,
        )
        copy.start()
        started.append(copy)
        return copy

    def spread(ref, size, between):
        def at(b, a, c):
            return ref.at[pl.ds(((b * 3 + a) * 3 + c) * size, size)]

        def along(axis, b, a, c):
            sides = {"gz": ((b, a, 0), (b, a, 2)), "gx": ((b, 0, c), (b, 2, c)), "gy": ((0, a, c), (2, a, c))}
            return [send(at(b, a, c), at(*side), axis, by) for side, by in zip(sides[axis], (1, -1))]

        def arrived(copies):
            for copy in copies:
                copy.wait_recv()

        in_z = along("gz", 1, 1, 1)
        in_x = along("gx", 1, 1, 1)
        in_y = along("gy", 1, 1, 1)
        between[0]()
        arrived(in_x)
        in_y += along("gy", 1, 0, 1) + along("gy", 1, 2, 1)
        arrived(in_z)
        in_x = along("gx", 1, 1, 0) + along("gx", 1, 1, 2)
        in_y += along("gy", 1, 1, 0) + along("gy", 1, 1, 2)
        between[1]()
        arrived(in_x)
        for c in (0, 2):
            in_y += along("gy", 1, 0, c) + along("gy", 1, 2, c)
        between[2]()
        arrived(in_y)

    loads[0].wait()
    loads[1].wait()
    lane = lax.broadcasted_iota(jnp.int32, (atoms, atoms), 0)
    kind_t = jnp.where(lane == species[...], 1.0, 0.0).astype(BF16)
    lend_t = jnp.where(
        lax.broadcasted_iota(jnp.int32, (atoms, sends), 0) == send_list[...], 1.0, 0.0
    ).astype(BF16)
    lend_wide = mm_nt(eye(128, sends), lend_t).astype(BF16)
    lend = lend_wide[:sends]
    species_rows = jnp.broadcast_to(species[...].astype(F32), (unit, atoms))
    kinds[pl.ds(13 * unit, unit), :] = mm_nt(species_rows.astype(BF16), lend_wide)
    pl.semaphore_wait(barrier, 6)

    def geometry():
        for load in loads[2:5]:
            load.wait()
        live = lax.broadcasted_iota(jnp.int32, (1, edges), 1) < edge_count[0, 0, 0]
        x = jnp.where(live, vectors[0], 1.0)
        y = jnp.where(live, vectors[1], 1.0)
        z = jnp.where(live, vectors[2], 1.0)
        square = x * x + y * y + z * z
        inverse = lax.rsqrt(square)
        distance = square * inverse
        ux, uy, uz = x * inverse, y * inverse, z * inverse
        for row, value in enumerate((ux, uy, uz, inverse)):
            geo[pl.ds(row, 1), :] = value
        for row, value in enumerate((
            ux, uy, uz, root * ux * uy, root * uy * uz, 0.5 * (3.0 * uz * uz - 1.0), root * ux * uz,
            0.5 * root * (ux * ux - uy * uy),
        )):
            harm[pl.ds(row, 1), :] = value
        sine, cosine = sin_cos(distance * (math.pi / CUTOFF))
        ratio = distance * (1.0 / CUTOFF)
        rest = 1.0 - ratio * ratio
        scale = rest * rest * inverse
        dscale = -(4.0 / CUTOFF) * rest * ratio * inverse - scale * inverse
        sin_k, cos_k = sine, cosine
        basis[...] = jnp.zeros_like(basis)
        for k in range(1, RADIAL + 1):
            basis[pl.ds(k - 1, 1), :] = sin_k * scale
            dbas[pl.ds(k - 1, 1), :] = (k * math.pi / CUTOFF) * cos_k * scale + sin_k * dscale
            sin_k, cos_k = sin_k * cosine + cos_k * sine, cos_k * cosine - sin_k * sine

        near = neighbour[...]
        ghost = near - atoms
        part_a = jnp.where(ghost >= rows_y, 1, 0) + jnp.where(ghost >= 2 * rows_y, 1, 0)
        ghost = ghost - rows_y * part_a
        part_b = jnp.where(ghost >= rows_x, 1, 0) + jnp.where(ghost >= 2 * rows_x, 1, 0)
        ghost = ghost - rows_x * part_b + rows_x * part_a + rows_y * part_b + atoms
        place = jnp.where(live, jnp.where(near < atoms, near, ghost), -1)
        middle = jnp.where(live, center[...], -1)
        block = lax.shift_right_arithmetic(place, sends.bit_length() - 1)
        slot = lax.bitwise_and(place, sends - 1)
        rows = lax.broadcasted_iota(jnp.int32, (32, edges), 0)
        block_of[...] = jnp.where(rows == block, 1.0, 0.0).astype(BF16)
        rows = lax.broadcasted_iota(jnp.int32, (atoms, edges), 0)
        slot_of[...] = jnp.where(rows == slot, 1.0, 0.0).astype(BF16)
        onehot_c[...] = jnp.where(rows == middle, 1.0, 0.0).astype(BF16)
        rows = lax.broadcasted_iota(jnp.int32, onehot.shape, 0)
        onehot[...] = jnp.where(rows == place, 1.0, 0.0).astype(BF16)

    def cut(i):
        return pl.ds(pl.multiple_of(i * TILE, TILE), TILE)

    def radial():
        for load in loads[5:]:
            load.wait()
        rad0_t = jnp.concatenate(
            [
                turned(
                    jnp.concatenate(
                        [w_rad0[l].astype(F32), jnp.zeros((8, w_rad0.shape[2]), F32)], axis=0
                    ).astype(BF16)
                ).astype(F32)
                for l in range(2)
            ],
            axis=0,
        ).astype(BF16)
        rad1_t1 = turned(w_rad1[0][:, : width + chan])
        rad1_t2 = turned(w_rad1[1][:, :width])

        def prepare(i, carry):
            span = cut(i)
            pre = mm(rad0_t, basis[:, span].astype(BF16))
            sig = jax.nn.sigmoid(pre)
            slope[:, span] = sig * (1.0 + pre * (1.0 - sig))
            hidden = (pre * sig).astype(BF16)
            rad1[:, span] = mm(rad1_t1, hidden[:hid])
            rad2[:, span] = mm(rad1_t2, hidden[hid:])
            return carry

        lax.fori_loop(0, tiles, prepare, 0)

    root = math.sqrt(3.0)
    hid = w_rad0.shape[2]
    spread(kinds, unit, (geometry, radial, lambda: None))
    src1_t = w_src[0]
    src2_t = w_src[1]
    src2 = turned(src2_t[:width])
    inv_t = turned(w_inv[1])
    out1_t = turned(w_out[0])
    out2_t = turned(w_out[1])
    gate_t = w_gate[0]
    embed_rows = jnp.concatenate([embed[...], jnp.zeros((16 - embed.shape[0], width), F32)], axis=0)
    embed_t = turned(embed_rows.astype(BF16))
    kind_proj = mm(src1_t, embed_t).astype(BF16)
    start = mm(embed_t, kind_t[:16, :])

    number = species_rows[:1]
    kind_rows = [number] + [pltpu.roll(number, atoms - j * sends, 1) for j in range(1, atoms // sends)]
    kind_rows += [kinds[pl.ds(i * unit, 1), :] for i in range(27)]
    kind_rows += [jnp.zeros((1, atoms), F32)] * (32 - blocks)
    kind_table = mm_nt(eye(sends, atoms), jnp.concatenate(kind_rows, axis=0).astype(BF16)).astype(BF16)
    agg[...] = jnp.zeros_like(agg)

    def layer_one(i, carry):
        span = cut(i)
        kind = sum_rows(mm(kind_table, block_of[:, span]) * slot_of[pl.ds(0, sends), span].astype(F32))
        kind_ids = lax.broadcasted_iota(jnp.int32, (16, TILE), 0).astype(F32)
        proj = mm(kind_proj, jnp.where(kind_ids == kind, 1.0, 0.0).astype(BF16))
        proj1[:, span] = proj
        lead_s = proj[:width] * rad1[pl.ds(0, width), span]
        lead_t = proj[width:] * rad1[pl.ds(width, chan), span]
        parts = [lead_s.astype(BF16)]
        for m in range(8):
            parts.append((lead_t * harm[pl.ds(m, 1), span]).astype(BF16))
        agg[...] += mm_nt(jnp.concatenate(parts, axis=0), onehot_c[:, span])
        return carry

    lax.fori_loop(0, tiles, layer_one, 0)
    gathered = 0.25 * agg[...]
    gathered_t = gathered[width:]
    rounded = gathered[:width].astype(BF16)
    pre1 = mm(out1_t, rounded)
    sig1 = jax.nn.sigmoid(pre1)
    gate = jax.nn.sigmoid(mm(gate_t, rounded))
    scalars = (start + pre1 * sig1).astype(BF16)
    gates = jnp.concatenate([gate] * 8, axis=0)
    tensors = (gathered_t * gates).astype(BF16)
    proj2 = mm(src2_t, scalars).astype(BF16)
    local = jnp.concatenate([proj2[:width], tensors], axis=0)
    halo[pl.ds(13 * sends, sends), :] = mm_nt(lend, local).astype(BF16)
    table[:, pl.ds(0, atoms)] = local
    nothing = lambda: None
    spread(halo, sends, (nothing, nothing, nothing))
    table[:, pl.ds(atoms, ghosts)] = halo[...].T
    agg2[...] = jnp.zeros_like(agg2)

    def layer_two(i, carry):
        span = cut(i)
        rows = mm(table[...], onehot[pl.ds(0, atoms + ghosts), span])
        picked[:, span] = rows.astype(BF16)
        inner = jnp.zeros((chan, TILE), F32)
        for m in range(8):
            inner += rows[width + m * chan : width + (m + 1) * chan] * harm[pl.ds(m, 1), span]
        message = rows[:width] * rad2[:, span] + mm(inv_t, inner.astype(BF16))
        agg2[...] += mm_nt(message.astype(BF16), onehot_c[:, span])
        return carry

    lax.fori_loop(0, tiles, layer_two, 0)
    rounded = (0.25 * agg2[...]).astype(BF16)
    pre2 = mm(out2_t, rounded)
    sig2 = jax.nn.sigmoid(pre2)
    readout = jnp.broadcast_to(w_energy[...], (width, width)).T[:, :1]
    mask = jnp.where(
        lax.broadcasted_iota(jnp.int32, (1, atoms), 1) < atom_count[0, 0, 0], 1.0, 0.0
    )
    energies[...] = mask * sum_rows((scalars.astype(F32) + pre2 * sig2) * readout)

    d_new = readout * mask
    d_pre = (d_new * sig2 * (1.0 + pre2 * (1.0 - sig2))).astype(BF16)
    d_agg = (0.25 * mm(w_out[1], d_pre).astype(BF16).astype(F32)).astype(BF16)

    def back_two(i, carry):
        span = cut(i)
        d_msg = mm(d_agg, onehot_c[:, span])
        dmsg[pl.ds(0, width), span] = (d_msg * rad2[:, span]).astype(BF16)
        d_inv = mm(w_inv[1], d_msg.astype(BF16))
        for m in range(8):
            dmsg[pl.ds(width + m * chan, chan), span] = (d_inv * harm[pl.ds(m, 1), span]).astype(BF16)
        return carry

    lax.fori_loop(0, tiles, back_two, 0)
    back_y = {}
    for slot, part, by in ((0, 0, -1), (1, 2, 1)):
        back_send_y[slot] = mm_nt(
            onehot[pl.ds(atoms + part * rows_y, rows_y), :], dmsg[...]
        ).astype(BF16)
        for a in (0, 2, 1):
            rows = pl.ds(a * rows_x, rows_x)
            back_y[slot, a] = send(back_send_y.at[slot, rows], back_recv_y.at[slot, rows], "gy", by)
    back = mm_nt(onehot[pl.ds(atoms + rows_y, rows_y), :], dmsg[...])
    d_local = mm_nt(dmsg[...], onehot[pl.ds(0, atoms), :])

    def edge_two(i, carry):
        span = cut(i)
        d_msg = mm(d_agg, onehot_c[:, span])
        d_inv = mm(w_inv[1], d_msg.astype(BF16))
        for m in range(8):
            grad_y[pl.ds(m, 1), span] = sum_rows(
                d_inv * picked[pl.ds(width + m * chan, chan), span].astype(F32)
            )
        d_rad = (d_msg * picked[pl.ds(0, width), span].astype(F32)).astype(BF16)
        d_hid = mm(w_rad1[1][:, :width], d_rad) * slope[pl.ds(hid, hid), span]
        d_bas = mm(w_rad0[1], d_hid.astype(BF16))
        grad_d[:, span] = sum_rows(d_bas * dbas[:, span])
        return carry

    lax.fori_loop(0, tiles, edge_two, 0)

    def merged(a):
        rows = pl.ds(a * rows_x, rows_x)
        for slot in range(2):
            back_y[slot, a].wait_recv()
        return (
            back[a * rows_x : (a + 1) * rows_x] + back_recv_y[0, rows].astype(F32) + back_recv_y[1, rows].astype(F32)
        )

    back_x = {}
    for slot, part, by in ((0, 0, -1), (1, 2, 1)):
        back_send_x[slot] = merged(part).astype(BF16)
        for c in (0, 2, 1):
            rows = pl.ds(c * sends, sends)
            back_x[slot, c] = send(back_send_x.at[slot, rows], back_recv_x.at[slot, rows], "gx", by)
    middle_rows = merged(1)

    def gathered_x(c):
        rows = pl.ds(c * sends, sends)
        for slot in range(2):
            back_x[slot, c].wait_recv()
        return (
            middle_rows[c * sends : (c + 1) * sends]
            + back_recv_x[0, rows].astype(F32) + back_recv_x[1, rows].astype(F32)
        )

    back_z = []
    for slot, part, by in ((0, 0, -1), (1, 2, 1)):
        back_send_z[slot] = gathered_x(part).astype(BF16)
        back_z.append(send(back_send_z.at[slot], back_recv_z.at[slot], "gz", by))
    back = gathered_x(1)
    for copy in back_z:
        copy.wait_recv()
    back = back + back_recv_z[0].astype(F32) + back_recv_z[1].astype(F32)
    owned = d_local + mm(back.T.astype(BF16), lend)

    d_scalars = (d_new + mm(src2, owned[:width].astype(BF16))).astype(BF16).astype(F32)
    d_tensors = owned[width:].astype(BF16).astype(F32)
    d_pre = (d_scalars * sig1 * (1.0 + pre1 * (1.0 - sig1))).astype(BF16)
    product = d_tensors * gathered_t
    d_gate = jnp.zeros((chan, atoms), F32)
    for m in range(8):
        d_gate += product[m * chan : (m + 1) * chan]
    d_gate = (d_gate * gate * (1.0 - gate)).astype(BF16)
    d_scalar_agg = (mm(w_out[0], d_pre) + mm(turned(gate_t), d_gate)).astype(BF16).astype(F32)
    d_agg1 = (0.25 * jnp.concatenate([d_scalar_agg, d_tensors * gates], axis=0)).astype(BF16)

    def edge_one(i, carry):
        span = cut(i)
        d_msg = mm(d_agg1, onehot_c[:, span])
        proj = proj1[:, span]
        lead_t = proj[width:] * rad1[pl.ds(width, chan), span]
        inner = jnp.zeros((chan, TILE), F32)
        gy = []
        for m in range(8):
            d_part = d_msg[width + m * chan : width + (m + 1) * chan]
            inner += d_part * harm[pl.ds(m, 1), span]
            gy.append(grad_y[pl.ds(m, 1), span] + sum_rows(d_part * lead_t))
        d_rad = jnp.concatenate([d_msg[:width], inner], axis=0) * proj
        d_hid = mm(w_rad1[0][:, : width + chan], d_rad.astype(BF16)) * slope[pl.ds(0, hid), span]
        d_bas = mm(w_rad0[0], d_hid.astype(BF16))
        gd = grad_d[:, span] + sum_rows(d_bas * dbas[:, span])
        ax, ay, az = geo[0:1, span], geo[1:2, span], geo[2:3, span]
        gux = gy[0] + root * (ay * gy[3] + az * gy[6] + ax * gy[7])
        guy = gy[1] + root * (ax * gy[3] + az * gy[4] - ay * gy[7])
        guz = gy[2] + root * (ay * gy[4] + ax * gy[6]) + 3.0 * az * gy[5]
        radial = gd - geo[3:4, span] * (ax * gux + ay * guy + az * guz)
        pull[pl.ds(0, 1), span] = geo[3:4, span] * gux + ax * radial
        pull[pl.ds(1, 1), span] = geo[3:4, span] * guy + ay * radial
        pull[pl.ds(2, 1), span] = geo[3:4, span] * guz + az * radial
        return carry

    pull[...] = jnp.zeros_like(pull)
    lax.fori_loop(0, tiles, edge_one, 0)

    pulls = pull[...]
    high = pulls.astype(BF16).astype(F32)
    pulls = high + pltpu.roll(pulls - high, 3, 0)
    f_rows = jnp.concatenate(
        [pulls * block_of[pl.ds(i, 1), :].astype(F32) for i in range(blocks)], axis=0
    ).astype(BF16)
    f_all[...] = mm_nt(f_rows, slot_of[...])
    first = (atoms // sends) * unit
    span_y, span_x = 9 * unit, 3 * unit
    f_y = [
        send(f_all.at[pl.ds(first + part * span_y, span_y)], f_recv_y.at[slot], "gy", by)
        for slot, part, by in ((0, 0, -1), (1, 2, 1))
    ]
    total = mm_nt(pulls.astype(BF16), onehot_c[...])
    for j in range(atoms // sends):
        block = f_all[pl.ds(j * unit, unit), :]
        total = total - (block if j == 0 else pltpu.roll(block, j * sends, 1))
    for copy in f_y:
        copy.wait_recv()
    lines = f_all[pl.ds(first + span_y, span_y), :] + f_recv_y[0] + f_recv_y[1]
    f_x = []
    for slot, part, by in ((0, 0, -1), (1, 2, 1)):
        f_send_x[slot] = lines[part * span_x : (part + 1) * span_x]
        f_x.append(send(f_send_x.at[slot], f_recv_x.at[slot], "gx", by))
    for copy in f_x:
        copy.wait_recv()
    lines = lines[span_x : 2 * span_x] + f_recv_x[0] + f_recv_x[1]
    f_z = []
    for slot, part, by in ((0, 0, -1), (1, 2, 1)):
        f_send_z[slot] = lines[part * unit : (part + 1) * unit]
        f_z.append(send(f_send_z.at[slot], f_recv_z.at[slot], "gz", by))
    for copy in f_z:
        copy.wait_recv()
    lines = lines[unit : 2 * unit] + f_recv_z[0] + f_recv_z[1]
    total = total - joined(mm(split(lines), lend_wide))
    for row in range(3):
        forces[row] = total[row : row + 1] + total[row + 3 : row + 4]
    for copy in started:
        copy.wait_send()


def per_device(
    species, atom_count, send_list, edge_count, edge_center, edge_neighbour, edge_vectors,
    embed, w_src, w_rad0, w_rad1, w_inv, w_out, w_gate, w_energy,
):
    atoms = species.shape[-1]
    edges = edge_center.shape[-1]
    sends = send_list.shape[-1]
    width = w_out.shape[1]
    chan = w_gate.shape[2]
    hid = w_rad0.shape[2]
    cols = width + 8 * chan
    ghosts = 27 * sends
    unit = 8
    vmem = pl.BlockSpec(memory_space=pltpu.VMEM)
    smem = pl.BlockSpec(memory_space=pltpu.SMEM)
    hbm = pl.BlockSpec(memory_space=pl.ANY)
    copies = 26 + 26 + 14 + 6
    operands = (
        species.reshape(1, atoms), send_list.reshape(1, sends), edge_vectors.reshape(3, 1, edges),
        edge_neighbour.reshape(1, edges), edge_center.reshape(1, edges),
        embed, jnp.swapaxes(w_src, 1, 2), w_rad0, w_rad1, w_inv, w_out, jnp.swapaxes(w_gate, 1, 2),
        w_energy.reshape(1, width),
    )
    energies, forces = pl.pallas_call(
        body,
        out_shape=(
            jax.ShapeDtypeStruct((1, atoms), F32),
            jax.ShapeDtypeStruct((3, 1, atoms), F32),
        ),
        in_specs=[smem, smem] + [hbm] * len(operands),
        out_specs=(vmem, vmem),
        scratch_shapes=[pltpu.VMEM(operand.shape, operand.dtype) for operand in operands] + [
            pltpu.VMEM((atoms + ghosts, edges), BF16),
            pltpu.VMEM((atoms, edges), BF16),
            pltpu.VMEM((32, edges), BF16),
            pltpu.VMEM((atoms, edges), BF16),
            pltpu.VMEM((27 * unit, atoms), F32),
            pltpu.VMEM((ghosts, cols), BF16),
            pltpu.VMEM((cols, atoms + ghosts), BF16),
            pltpu.VMEM((cols, edges), BF16),
            pltpu.VMEM((cols, edges), BF16),
            pltpu.VMEM((8, edges), F32),
            pltpu.VMEM((8, edges), F32),
            pltpu.VMEM((8, edges), F32),
            pltpu.VMEM((16, edges), F32),
            pltpu.VMEM((2 * hid, edges), F32),
            pltpu.VMEM((width + chan, edges), F32),
            pltpu.VMEM((width, edges), F32),
            pltpu.VMEM((width + chan, edges), F32),
            pltpu.VMEM((cols, atoms), F32),
            pltpu.VMEM((width, atoms), F32),
            pltpu.VMEM((8, edges), F32),
            pltpu.VMEM((1, edges), F32),
            pltpu.VMEM((8, edges), F32),
            pltpu.VMEM((2, 9 * sends, cols), BF16),
            pltpu.VMEM((2, 9 * sends, cols), BF16),
            pltpu.VMEM((2, 3 * sends, cols), BF16),
            pltpu.VMEM((2, 3 * sends, cols), BF16),
            pltpu.VMEM((2, sends, cols), BF16),
            pltpu.VMEM((2, sends, cols), BF16),
            pltpu.VMEM(((atoms // sends + 27) * unit, 128), F32),
            pltpu.VMEM((2, 9 * unit, 128), F32),
            pltpu.VMEM((2, 3 * unit, 128), F32),
            pltpu.VMEM((2, 3 * unit, 128), F32),
            pltpu.VMEM((2, unit, 128), F32),
            pltpu.VMEM((2, unit, 128), F32),
            pltpu.SemaphoreType.DMA((copies,)),
            pltpu.SemaphoreType.DMA((copies,)),
            pltpu.SemaphoreType.DMA((len(operands),)),
        ],
        compiler_params=pltpu.CompilerParams(
            collective_id=0, has_side_effects=True, vmem_limit_bytes=56 * 1024 * 1024
        ),
    )(atom_count, edge_count, *operands)
    return energies.reshape(species.shape), forces.reshape(edge_vectors.shape[:3] + (3, atoms))


def solution(mesh):
    shard = P("gx", "gy", "gz", None)
    count = P("gx", "gy", "gz")
    wide = P("gx", "gy", "gz", None, None)
    return jax.shard_map(
        per_device,
        mesh=mesh,
        in_specs=(shard, count, shard, count, shard, shard, wide) + (P(),) * 8,
        out_specs=(shard, wide),
        check_vma=False,
    )
```

```python
import functools
import math

import jax
import jax.numpy as jnp
from jax import lax
from jax.experimental import pallas as pl
from jax.experimental.pallas import tpu as pltpu
from jax.sharding import PartitionSpec as P

RADIAL = 8
CUTOFF = 5.0
PLANE = ((1, 0), (1, 1), (1, 2), (0, 1), (2, 1), (0, 0), (0, 2), (2, 0), (2, 2))
REST = 5


def position(b, a, c):
    index = PLANE.index((c, a))
    if b == 1:
        return index
    if index < REST:
        return 9 + (b // 2) * REST + index
    return 9 + 2 * REST + (b // 2) * (9 - REST) + index - REST


MESH = pl.DeviceIdType.MESH
BF16 = jnp.bfloat16
F32 = jnp.float32


def mm(left, right):
    return lax.dot_general(left, right, (((1,), (0,)), ((), ())), preferred_element_type=F32)


def mm_nt(left, right):
    return lax.dot_general(left, right, (((1,), (1,)), ((), ())), preferred_element_type=F32)


def eye(rows, cols):
    first = lax.broadcasted_iota(jnp.int32, (rows, cols), 0)
    second = lax.broadcasted_iota(jnp.int32, (rows, cols), 1)
    return jnp.where(first == second, 1.0, 0.0).astype(BF16)


def turned(array):
    return mm_nt(eye(array.shape[1], array.shape[1]), array).astype(BF16)


def split(array):
    high = array.astype(BF16).astype(F32)
    return jnp.concatenate([high, array - high], axis=0).astype(BF16)


def joined(array):
    half = array.shape[0] // 2
    return array[:half] + array[half:]


def sum_rows(array):
    return jnp.sum(array, axis=0, keepdims=True)


def sin_cos(angle):
    y = angle - (math.pi / 2)
    y2 = y * y
    sin_y = jnp.full_like(y, -1.0 / math.factorial(11))
    for power in (9, 7, 5, 3, 1):
        sin_y = sin_y * y2 + ((-1.0) ** (power // 2)) / math.factorial(power)
    cos_y = jnp.full_like(y, 1.0 / math.factorial(12))
    for power in (10, 8, 6, 4, 2, 0):
        cos_y = cos_y * y2 + ((-1.0) ** (power // 2)) / math.factorial(power)
    return cos_y, -(sin_y * y)


def body(
    atom_count, edge_count, *refs
):
    args, (energies, forces), held = refs[:13], refs[13:15], refs[15:28]
    (
        onehot, onehot_c, block_of, slot_of, kinds, halo, table, last_table, picked, dmsg,
        geo, harm, dbas, basis, slope, rad1, rad2, proj1, src2, gate_w, inv_t, out_t, kind_proj, start, readout, f_rows, agg, agg2, grad_y, grad_d, pull,
        back_send_y, back_recv_y, back_send_x, back_recv_x, back_send_z, back_recv_z,
        f_all, f_recv_y, f_send_x, f_recv_x, f_send_z, f_recv_z,
        send_sems, recv_sems, arg_sems,
    ) = refs[28:]
    (
        species, send_list, vectors, neighbour, center,
        embed, w_src, w_rad0, w_rad1, w_inv, w_out, w_gate, w_energy,
    ) = held
    atoms = species.shape[1]
    edges = center.shape[1]
    sends = send_list.shape[1]
    width = w_out.shape[1]
    chan = w_gate.shape[1]
    rows_y = 9 * sends
    rest = REST * sends
    corner = 9 * sends - rest
    early = atoms + 27 * sends - 2 * corner
    unit = 8
    blocks = atoms // sends + 27

    def step(axis, by):
        size = lax.axis_size(axis)
        return {axis: lax.rem(lax.axis_index(axis) + size + by, size)}

    barrier = pltpu.get_barrier_semaphore()
    for axis in ("gx", "gy", "gz"):
        for by in (1, -1):
            pl.semaphore_signal(barrier, inc=1, device_id=step(axis, by), device_id_type=MESH)

    loads = [
        pltpu.make_async_copy(source, target, arg_sems.at[i])
        for i, (source, target) in enumerate(zip(args, held))
    ]
    for load in loads:
        load.start()

    next_sem = [0]
    started = []

    def send(source, target, axis, by):
        slot = next_sem[0]
        next_sem[0] = slot + 1
        copy = pltpu.make_async_remote_copy(
            src_ref=source, dst_ref=target, send_sem=send_sems.at[slot], recv_sem=recv_sems.at[slot],
            device_id=step(axis, by), device_id_type=MESH,
        )
        copy.start()
        started.append(copy)
        return copy

    def spread(ref, size, between):
        def at(b, a, c):
            return ref.at[pl.ds(position(b, a, c) * size, size)]

        def along(axis, b, a, c):
            sides = {"gz": ((b, a, 0), (b, a, 2)), "gx": ((b, 0, c), (b, 2, c)), "gy": ((0, a, c), (2, a, c))}
            return [send(at(b, a, c), at(*side), axis, by) for side, by in zip(sides[axis], (1, -1))]

        def arrived(copies):
            for copy in copies:
                copy.wait_recv()

        in_z = along("gz", 1, 1, 1)
        in_x = along("gx", 1, 1, 1)
        in_y = along("gy", 1, 1, 1)
        between[0]()
        arrived(in_x)
        in_y += along("gy", 1, 0, 1) + along("gy", 1, 2, 1)
        arrived(in_z)
        in_x = along("gx", 1, 1, 0) + along("gx", 1, 1, 2)
        in_y += along("gy", 1, 1, 0) + along("gy", 1, 1, 2)
        between[1]()
        arrived(in_x)
        last = []
        for c in (0, 2):
            last += along("gy", 1, 0, c) + along("gy", 1, 2, c)
        arrived(in_y)
        between[2]()
        arrived(last)

    loads[0].wait()
    loads[1].wait()
    lane = lax.broadcasted_iota(jnp.int32, (atoms, atoms), 0)
    kind_t = jnp.where(lane == species[...], 1.0, 0.0).astype(BF16)
    lend_t = jnp.where(
        lax.broadcasted_iota(jnp.int32, (atoms, sends), 0) == send_list[...], 1.0, 0.0
    ).astype(BF16)
    lend_wide = mm_nt(eye(128, sends), lend_t).astype(BF16)
    lend = lend_wide[:sends]
    species_rows = jnp.broadcast_to(species[...].astype(F32), (unit, atoms))
    kinds[pl.ds(position(1, 1, 1) * unit, unit), :] = mm_nt(species_rows.astype(BF16), lend_wide)
    pl.semaphore_wait(barrier, 6)


    def geometry():
        for load in loads[2:5]:
            load.wait()
        live = lax.broadcasted_iota(jnp.int32, (1, edges), 1) < edge_count[0, 0, 0]
        x = jnp.where(live, vectors[0], 1.0)
        y = jnp.where(live, vectors[1], 1.0)
        z = jnp.where(live, vectors[2], 1.0)
        square = x * x + y * y + z * z
        inverse = lax.rsqrt(square)
        distance = square * inverse
        ux, uy, uz = x * inverse, y * inverse, z * inverse
        for row, value in enumerate((ux, uy, uz, inverse)):
            geo[pl.ds(row, 1), :] = value
        for row, value in enumerate((
            ux, uy, uz, root * ux * uy, root * uy * uz, 0.5 * (3.0 * uz * uz - 1.0), root * ux * uz,
            0.5 * root * (ux * ux - uy * uy),
        )):
            harm[pl.ds(row, 1), :] = value
        sine, cosine = sin_cos(distance * (math.pi / CUTOFF))
        ratio = distance * (1.0 / CUTOFF)
        rest = 1.0 - ratio * ratio
        scale = rest * rest * inverse
        dscale = -(4.0 / CUTOFF) * rest * ratio * inverse - scale * inverse
        sin_k, cos_k = sine, cosine
        basis[...] = jnp.zeros_like(basis)
        for k in range(1, RADIAL + 1):
            basis[pl.ds(k - 1, 1), :] = sin_k * scale
            dbas[pl.ds(k - 1, 1), :] = (k * math.pi / CUTOFF) * cos_k * scale + sin_k * dscale
            sin_k, cos_k = sin_k * cosine + cos_k * sine, cos_k * cosine - sin_k * sine

        place = jnp.where(live, neighbour[...], -1)
        middle = jnp.where(live, center[...], -1)
        block = lax.shift_right_arithmetic(place, sends.bit_length() - 1)
        slot = lax.bitwise_and(place, sends - 1)
        order = {position(b, a, c): (a * 3 + b) * 3 + c for a in range(3) for b in range(3) for c in range(3)}
        rows = lax.broadcasted_iota(jnp.int32, (32, 1), 0)
        block_ids = rows
        for i in range(27):
            block_ids = jnp.where(rows == atoms // sends + i, atoms // sends + order[i], block_ids)
        block_of[...] = jnp.where(block_ids == block, 1.0, 0.0).astype(BF16)
        rows = lax.broadcasted_iota(jnp.int32, (atoms, edges), 0)
        slot_of[...] = jnp.where(rows == slot, 1.0, 0.0).astype(BF16)
        onehot_c[...] = jnp.where(rows == middle, 1.0, 0.0).astype(BF16)
        onehot[pl.ds(0, atoms), :] = jnp.where(rows == place, 1.0, 0.0).astype(BF16)
        rows = lax.broadcasted_iota(jnp.int32, (sends, edges), 0)
        for i in range(27):
            onehot[pl.ds(atoms + i * sends, sends), :] = jnp.where(
                rows == place - (atoms + order[i] * sends), 1.0, 0.0
            ).astype(BF16)

    def sweep(tile, work):
        if tile < 0:
            for i in range(edges // -tile):
                work(pl.ds(i * -tile, -tile))
        elif tile == edges:
            work(pl.ds(0, edges))
        else:
            lax.fori_loop(
                0, edges // tile, lambda i, carry: (work(pl.ds(pl.multiple_of(i * tile, tile), tile)), carry)[1], 0
            )

    def radial():
        for load in loads[5:]:
            load.wait()
        rad0_t = jnp.concatenate(
            [
                turned(
                    jnp.concatenate(
                        [w_rad0[l].astype(F32), jnp.zeros((8, w_rad0.shape[2]), F32)], axis=0
                    ).astype(BF16)
                ).astype(F32)
                for l in range(2)
            ],
            axis=0,
        ).astype(BF16)
        rad1_t1 = turned(w_rad1[0][:, : width + chan])
        rad1_t2 = turned(w_rad1[1][:, :width])

        def prepare(span):
            pre = mm(rad0_t, basis[:, span].astype(BF16))
            sig = jax.nn.sigmoid(pre)
            slope[:, span] = sig * (1.0 + pre * (1.0 - sig))
            hidden = (pre * sig).astype(BF16)
            rad1[:, span] = mm(rad1_t1, hidden[:hid])
            rad2[:, span] = mm(rad1_t2, hidden[hid:])

        sweep(edges, prepare)

        src2[...] = turned(w_src[1][:width])
        gate_w[...] = turned(w_gate[0])
        inv_t[...] = turned(w_inv[1])
        for layer in range(2):
            out_t[layer] = turned(w_out[layer])
        embed_rows = jnp.concatenate([embed[...], jnp.zeros((16 - embed.shape[0], width), F32)], axis=0)
        embed_t = turned(embed_rows.astype(BF16))
        kind_proj[...] = mm(w_src[0], embed_t).astype(BF16)
        start[...] = mm(embed_t, kind_t[:16, :])
        readout[...] = jnp.broadcast_to(w_energy[...], (width, width)).T

    root = math.sqrt(3.0)
    hid = w_rad0.shape[2]
    spread(kinds, unit, (geometry, radial, lambda: None))
    number = species_rows[:1]
    kind_rows = [number] + [pltpu.roll(number, atoms - j * sends, 1) for j in range(1, atoms // sends)]
    kind_rows += [kinds[pl.ds(i * unit, 1), :] for i in range(27)]
    kind_rows += [jnp.zeros((1, atoms), F32)] * (32 - blocks)
    kind_table = mm_nt(eye(sends, atoms), jnp.concatenate(kind_rows, axis=0).astype(BF16)).astype(BF16)

    def layer_one(span):
        kind = sum_rows(mm(kind_table, block_of[:, span]) * slot_of[pl.ds(0, sends), span].astype(F32))
        kind_ids = lax.broadcasted_iota(jnp.int32, (16, kind.shape[1]), 0).astype(F32)
        proj = mm(kind_proj[...], jnp.where(kind_ids == kind, 1.0, 0.0).astype(BF16))
        proj1[:, span] = proj
        lead_s = proj[:width] * rad1[pl.ds(0, width), span]
        lead_t = proj[width:] * rad1[pl.ds(width, chan), span]
        parts = [lead_s.astype(BF16)]
        for m in range(8):
            parts.append((lead_t * harm[pl.ds(m, 1), span]).astype(BF16))
        agg[...] = mm_nt(jnp.concatenate(parts, axis=0), onehot_c[:, span])

    sweep(edges, layer_one)
    gathered = 0.25 * agg[...]
    gathered_t = gathered[width:]
    rounded = gathered[:width].astype(BF16)
    pre1 = mm(out_t[0], rounded)
    sig1 = jax.nn.sigmoid(pre1)
    gate = jax.nn.sigmoid(mm(w_gate[0], rounded))
    scalars = (start[...] + pre1 * sig1).astype(BF16)
    gates = jnp.concatenate([gate] * 8, axis=0)
    tensors = (gathered_t * gates).astype(BF16)
    proj2 = mm(w_src[1], scalars).astype(BF16)
    local = jnp.concatenate([proj2[:width], tensors], axis=0)
    halo[pl.ds(position(1, 1, 1) * sends, sends), :] = mm_nt(lend, local).astype(BF16)
    table[:, pl.ds(0, atoms)] = local
    nothing = lambda: None

    def lookup(span):
        picked[:, span] = mm(table[...], onehot[pl.ds(0, early), span]).astype(BF16)

    def early_rows():
        table[:, pl.ds(atoms, early - atoms)] = halo[pl.ds(0, early - atoms), :].T
        sweep(edges, lookup)

    spread(halo, sends, (nothing, nothing, early_rows))
    last_table[...] = halo[pl.ds(early - atoms, 2 * corner), :].T

    def layer_two(span):
        rows = picked[:, span].astype(F32) + mm(last_table[...], onehot[pl.ds(early, 2 * corner), span])
        picked[:, span] = rows.astype(BF16)
        inner = jnp.zeros((chan, span.size), F32)
        for m in range(8):
            inner += rows[width + m * chan : width + (m + 1) * chan] * harm[pl.ds(m, 1), span]
        message = rows[:width] * rad2[:, span] + mm(inv_t[...], inner.astype(BF16))
        agg2[...] = mm_nt(message.astype(BF16), onehot_c[:, span])

    sweep(edges, layer_two)
    rounded = (0.25 * agg2[...]).astype(BF16)
    pre2 = mm(out_t[1], rounded)
    sig2 = jax.nn.sigmoid(pre2)
    mask = jnp.where(
        lax.broadcasted_iota(jnp.int32, (1, atoms), 1) < atom_count[0, 0, 0], 1.0, 0.0
    )
    energies[...] = mask * sum_rows((scalars.astype(F32) + pre2 * sig2) * readout[...])

    d_new = readout[...] * mask
    d_pre = (d_new * sig2 * (1.0 + pre2 * (1.0 - sig2))).astype(BF16)
    d_agg = (0.25 * mm(w_out[1], d_pre).astype(BF16).astype(F32)).astype(BF16)

    def back_two(span):
        d_msg = mm(d_agg, onehot_c[:, span])
        dmsg[pl.ds(0, width), span] = (d_msg * rad2[:, span]).astype(BF16)
        d_inv = mm(w_inv[1], d_msg.astype(BF16))
        for m in range(8):
            dmsg[pl.ds(width + m * chan, chan), span] = (d_inv * harm[pl.ds(m, 1), span]).astype(BF16)

    sweep(edges, back_two)
    back_y = {}
    parity = lax.rem(lax.axis_index("gy"), 2)
    for slot, by in ((0, 2 * parity - 1), (1, 1 - 2 * parity)):
        side = (by + 1) // 2
        for piece, first, size, count in ((1, 9 * sends + 2 * rest, corner, corner), (0, 9 * sends, rest, rest)):
            rows = pl.ds(rest if piece else 0, size)
            start_row = pl.multiple_of(atoms + first + side * count, sends)
            back_send_y[slot, rows] = mm_nt(onehot[pl.ds(start_row, size), :], dmsg[...]).astype(BF16)
            back_y[slot, piece] = send(back_send_y.at[slot, rows], back_recv_y.at[slot, rows], "gy", by)
    back = mm_nt(onehot[pl.ds(atoms, rows_y), :], dmsg[...])
    d_local = mm_nt(dmsg[...], onehot[pl.ds(0, atoms), :])

    def edge_two(span):
        d_msg = mm(d_agg, onehot_c[:, span])
        d_inv = mm(w_inv[1], d_msg.astype(BF16))
        for m in range(8):
            grad_y[pl.ds(m, 1), span] = sum_rows(
                d_inv * picked[pl.ds(width + m * chan, chan), span].astype(F32)
            )
        d_rad = (d_msg * picked[pl.ds(0, width), span].astype(F32)).astype(BF16)
        d_hid = mm(w_rad1[1][:, :width], d_rad) * slope[pl.ds(hid, hid), span]
        d_bas = mm(w_rad0[1], d_hid.astype(BF16))
        grad_d[:, span] = sum_rows(d_bas * dbas[:, span])

    sweep(edges, edge_two)

    def merged(piece):
        rows = pl.ds(rest if piece else 0, corner if piece else rest)
        for slot in range(2):
            back_y[slot, piece].wait_recv()
        return (
            back[rows.start : rows.start + rows.size]
            + back_recv_y[0, rows].astype(F32) + back_recv_y[1, rows].astype(F32)
        )

    back_x = {}
    plane = {}
    for piece in (1, 0):
        sums = merged(piece)
        for i, (c, a) in enumerate(PLANE[REST:] if piece else PLANE[:REST]):
            plane[c, a] = sums[i * sends : (i + 1) * sends]
        for c in (0, 2) if piece else (1,):
            for slot, part, by in ((0, 0, -1), (1, 2, 1)):
                rows = pl.ds(c * sends, sends)
                back_send_x[slot, rows] = plane[c, part].astype(BF16)
                back_x[slot, c] = send(back_send_x.at[slot, rows], back_recv_x.at[slot, rows], "gx", by)

    def gathered_x(c):
        rows = pl.ds(c * sends, sends)
        for slot in range(2):
            back_x[slot, c].wait_recv()
        return plane[c, 1] + back_recv_x[0, rows].astype(F32) + back_recv_x[1, rows].astype(F32)

    back_z = []
    for slot, part, by in ((0, 0, -1), (1, 2, 1)):
        back_send_z[slot] = gathered_x(part).astype(BF16)
        back_z.append(send(back_send_z.at[slot], back_recv_z.at[slot], "gz", by))
    back = gathered_x(1)
    for copy in back_z:
        copy.wait_recv()
    back = back + back_recv_z[0].astype(F32) + back_recv_z[1].astype(F32)
    owned = d_local + mm(back.T.astype(BF16), lend)

    d_scalars = (d_new + mm(src2[...], owned[:width].astype(BF16))).astype(BF16).astype(F32)
    d_tensors = owned[width:].astype(BF16).astype(F32)
    d_pre = (d_scalars * sig1 * (1.0 + pre1 * (1.0 - sig1))).astype(BF16)
    product = d_tensors * gathered_t
    d_gate = jnp.zeros((chan, atoms), F32)
    for m in range(8):
        d_gate += product[m * chan : (m + 1) * chan]
    d_gate = (d_gate * gate * (1.0 - gate)).astype(BF16)
    d_scalar_agg = (mm(w_out[0], d_pre) + mm(gate_w[...], d_gate)).astype(BF16).astype(F32)
    d_agg1 = (0.25 * jnp.concatenate([d_scalar_agg, d_tensors * gates], axis=0)).astype(BF16)

    def edge_one(span):
        d_msg = mm(d_agg1, onehot_c[:, span])
        proj = proj1[:, span]
        lead_t = proj[width:] * rad1[pl.ds(width, chan), span]
        inner = jnp.zeros((chan, span.size), F32)
        gy = []
        for m in range(8):
            d_part = d_msg[width + m * chan : width + (m + 1) * chan]
            inner += d_part * harm[pl.ds(m, 1), span]
            gy.append(grad_y[pl.ds(m, 1), span] + sum_rows(d_part * lead_t))
        d_rad = jnp.concatenate([d_msg[:width], inner], axis=0) * proj
        d_hid = mm(w_rad1[0][:, : width + chan], d_rad.astype(BF16)) * slope[pl.ds(0, hid), span]
        d_bas = mm(w_rad0[0], d_hid.astype(BF16))
        gd = grad_d[:, span] + sum_rows(d_bas * dbas[:, span])
        ax, ay, az = geo[0:1, span], geo[1:2, span], geo[2:3, span]
        gux = gy[0] + root * (ay * gy[3] + az * gy[6] + ax * gy[7])
        guy = gy[1] + root * (ax * gy[3] + az * gy[4] - ay * gy[7])
        guz = gy[2] + root * (ay * gy[4] + ax * gy[6]) + 3.0 * az * gy[5]
        radial = gd - geo[3:4, span] * (ax * gux + ay * guy + az * guz)
        pull[pl.ds(0, 1), span] = geo[3:4, span] * gux + ax * radial
        pull[pl.ds(1, 1), span] = geo[3:4, span] * guy + ay * radial
        pull[pl.ds(2, 1), span] = geo[3:4, span] * guz + az * radial

    pull[...] = jnp.zeros_like(pull)
    sweep(edges, edge_one)

    pulls = pull[...]
    high = pulls.astype(BF16).astype(F32)
    pulls = high + pltpu.roll(pulls - high, 3, 0)
    for i in range(0, 32, 2):
        f_rows[pl.ds(i * unit, 2 * unit), :] = jnp.concatenate(
            [pulls * block_of[pl.ds(j, 1), :].astype(F32) for j in (i, i + 1)], axis=0
        ).astype(BF16)
    f_all[...] = mm_nt(f_rows[...], slot_of[...])
    first = (atoms // sends) * unit
    f_y = []
    for slot, part, by in ((0, 0, -1), (1, 2, 1)):
        for index, count in ((REST, 9 - REST), (0, REST)):
            c, a = PLANE[index]
            f_y.append(send(
                f_all.at[pl.ds(first + position(part, a, c) * unit, count * unit)],
                f_recv_y.at[slot, pl.ds(index * unit, count * unit)], "gy", by,
            ))
    total = mm_nt(pulls.astype(BF16), onehot_c[...])
    for j in range(atoms // sends):
        block = f_all[pl.ds(j * unit, unit), :]
        total = total - (block if j == 0 else pltpu.roll(block, j * sends, 1))
    for copy in f_y:
        copy.wait_recv()
    lines = f_all[pl.ds(first, 9 * unit), :] + f_recv_y[0] + f_recv_y[1]
    cells = {cell: lines[i * unit : (i + 1) * unit] for i, cell in enumerate(PLANE)}
    f_x = []
    for slot, part, by in ((0, 0, -1), (1, 2, 1)):
        f_send_x[slot] = jnp.concatenate([cells[c, part] for c in range(3)], axis=0)
        f_x.append(send(f_send_x.at[slot], f_recv_x.at[slot], "gx", by))
    for copy in f_x:
        copy.wait_recv()
    lines = jnp.concatenate([cells[c, 1] for c in range(3)], axis=0) + f_recv_x[0] + f_recv_x[1]
    f_z = []
    for slot, part, by in ((0, 0, -1), (1, 2, 1)):
        f_send_z[slot] = lines[part * unit : (part + 1) * unit]
        f_z.append(send(f_send_z.at[slot], f_recv_z.at[slot], "gz", by))
    for copy in f_z:
        copy.wait_recv()
    lines = lines[unit : 2 * unit] + f_recv_z[0] + f_recv_z[1]
    total = total - joined(mm(split(lines), lend_wide))
    for row in range(3):
        forces[row] = total[row : row + 1] + total[row + 3 : row + 4]
    for copy in started:
        copy.wait_send()


def per_device(
    species, atom_count, send_list, edge_count, edge_center, edge_neighbour, edge_vectors,
    embed, w_src, w_rad0, w_rad1, w_inv, w_out, w_gate, w_energy,
):
    atoms = species.shape[-1]
    edges = edge_center.shape[-1]
    sends = send_list.shape[-1]
    width = w_out.shape[1]
    chan = w_gate.shape[2]
    hid = w_rad0.shape[2]
    cols = width + 8 * chan
    ghosts = 27 * sends
    unit = 8
    early = atoms + (9 + 2 * REST) * sends
    vmem = pl.BlockSpec(memory_space=pltpu.VMEM)
    smem = pl.BlockSpec(memory_space=pltpu.SMEM)
    hbm = pl.BlockSpec(memory_space=pltpu.HBM)
    copies = 26 + 26 + 12 + 8
    operands = (
        species.reshape(1, atoms), send_list.reshape(1, sends), edge_vectors.reshape(3, 1, edges),
        edge_neighbour.reshape(1, edges), edge_center.reshape(1, edges),
        embed, jnp.swapaxes(w_src, 1, 2), w_rad0, w_rad1, w_inv, w_out, jnp.swapaxes(w_gate, 1, 2),
        w_energy.reshape(1, width),
    )
    energies, forces = pl.pallas_call(
        body,
        out_shape=(
            jax.ShapeDtypeStruct((1, atoms), F32),
            jax.ShapeDtypeStruct((3, 1, atoms), F32),
        ),
        in_specs=[smem, smem] + [hbm] * len(operands),
        out_specs=(vmem, vmem),
        scratch_shapes=[pltpu.VMEM(operand.shape, operand.dtype) for operand in operands] + [
            pltpu.VMEM((atoms + ghosts, edges), BF16),
            pltpu.VMEM((atoms, edges), BF16),
            pltpu.VMEM((32, edges), BF16),
            pltpu.VMEM((atoms, edges), BF16),
            pltpu.VMEM((27 * unit, atoms), F32),
            pltpu.VMEM((ghosts, cols), BF16),
            pltpu.VMEM((cols, early), BF16),
            pltpu.VMEM((cols, ghosts + atoms - early), BF16),
            pltpu.VMEM((cols, edges), BF16),
            pltpu.VMEM((cols, edges), BF16),
            pltpu.VMEM((8, edges), F32),
            pltpu.VMEM((8, edges), F32),
            pltpu.VMEM((8, edges), F32),
            pltpu.VMEM((16, edges), F32),
            pltpu.VMEM((2 * hid, edges), F32),
            pltpu.VMEM((width + chan, edges), F32),
            pltpu.VMEM((width, edges), F32),
            pltpu.VMEM((width + chan, edges), F32),
            pltpu.VMEM((width, width), BF16),
            pltpu.VMEM((width, chan), BF16),
            pltpu.VMEM((width, chan), BF16),
            pltpu.VMEM((2, width, width), BF16),
            pltpu.VMEM((width + chan, 16), BF16),
            pltpu.VMEM((width, atoms), F32),
            pltpu.VMEM((width, width), F32),
            pltpu.VMEM((32 * unit, edges), BF16),
            pltpu.VMEM((cols, atoms), F32),
            pltpu.VMEM((width, atoms), F32),
            pltpu.VMEM((8, edges), F32),
            pltpu.VMEM((1, edges), F32),
            pltpu.VMEM((8, edges), F32),
            pltpu.VMEM((2, 9 * sends, cols), BF16),
            pltpu.VMEM((2, 9 * sends, cols), BF16),
            pltpu.VMEM((2, 3 * sends, cols), BF16),
            pltpu.VMEM((2, 3 * sends, cols), BF16),
            pltpu.VMEM((2, sends, cols), BF16),
            pltpu.VMEM((2, sends, cols), BF16),
            pltpu.VMEM((32 * unit, 128), F32),
            pltpu.VMEM((2, 9 * unit, 128), F32),
            pltpu.VMEM((2, 3 * unit, 128), F32),
            pltpu.VMEM((2, 3 * unit, 128), F32),
            pltpu.VMEM((2, unit, 128), F32),
            pltpu.VMEM((2, unit, 128), F32),
            pltpu.SemaphoreType.DMA((copies,)),
            pltpu.SemaphoreType.DMA((copies,)),
            pltpu.SemaphoreType.DMA((len(operands),)),
        ],
        compiler_params=pltpu.CompilerParams(
            collective_id=0, has_side_effects=True, vmem_limit_bytes=56 * 1024 * 1024
        ),
    )(atom_count, edge_count, *operands)
    return energies.reshape(species.shape), forces.reshape(edge_vectors.shape[:3] + (3, atoms))


def solution(mesh):
    shard = P("gx", "gy", "gz", None)
    count = P("gx", "gy", "gz")
    wide = P("gx", "gy", "gz", None, None)
    return jax.shard_map(
        per_device,
        mesh=mesh,
        in_specs=(shard, count, shard, count, shard, shard, wide) + (P(),) * 8,
        out_specs=(shard, wide),
        check_vma=False,
    )
```

```python
import functools
import math

import jax
import jax.numpy as jnp
from jax import lax
from jax.experimental import pallas as pl
from jax.experimental.pallas import tpu as pltpu
from jax.sharding import PartitionSpec as P

RADIAL = 8
CUTOFF = 5.0
PLANE = ((1, 0), (1, 1), (1, 2), (0, 1), (2, 1), (0, 0), (0, 2), (2, 0), (2, 2))
REST = 5
OTHER, OWN, MATE = 0, 1, 2


def position(b, a, c):
    index = PLANE.index((c, a))
    if b == OWN:
        return index
    if index < REST:
        return 9 + (b // 2) * REST + index
    return 9 + 2 * REST + (b // 2) * (9 - REST) + index - REST


MESH = pl.DeviceIdType.MESH
BF16 = jnp.bfloat16
F32 = jnp.float32


def mm(left, right):
    return lax.dot_general(left, right, (((1,), (0,)), ((), ())), preferred_element_type=F32)


def mm_nt(left, right):
    return lax.dot_general(left, right, (((1,), (1,)), ((), ())), preferred_element_type=F32)


def eye(rows, cols):
    first = lax.broadcasted_iota(jnp.int32, (rows, cols), 0)
    second = lax.broadcasted_iota(jnp.int32, (rows, cols), 1)
    return jnp.where(first == second, 1.0, 0.0).astype(BF16)


def turned(array):
    return mm_nt(eye(array.shape[1], array.shape[1]), array).astype(BF16)


def split(array):
    high = array.astype(BF16).astype(F32)
    return jnp.concatenate([high, array - high], axis=0).astype(BF16)


def joined(array):
    half = array.shape[0] // 2
    return array[:half] + array[half:]


def sum_rows(array):
    return jnp.sum(array, axis=0, keepdims=True)


def sin_cos(angle):
    y = angle - (math.pi / 2)
    y2 = y * y
    sin_y = jnp.full_like(y, -1.0 / math.factorial(11))
    for power in (9, 7, 5, 3, 1):
        sin_y = sin_y * y2 + ((-1.0) ** (power // 2)) / math.factorial(power)
    cos_y = jnp.full_like(y, 1.0 / math.factorial(12))
    for power in (10, 8, 6, 4, 2, 0):
        cos_y = cos_y * y2 + ((-1.0) ** (power // 2)) / math.factorial(power)
    return cos_y, -(sin_y * y)


def body(
    atom_count, edge_count, *refs
):
    args, (energies, forces), held = refs[:13], refs[13:15], refs[15:28]
    (
        onehot, onehot_c, block_of, slot_of, kinds, halo, table, last_table, picked, dmsg,
        geo, harm, dbas, basis, slope, rad1, rad2, proj1, src2, gate_w, inv_t, out_t, kind_proj, start, readout, f_rows, agg, agg2, grad_y, grad_d, pull,
        back_send_o, back_recv_o, back_send_m, back_recv_m, back_send_x, back_recv_x, back_send_z, back_recv_z,
        f_all, f_send_o, f_recv_o, f_send_m, f_recv_m, f_send_x, f_recv_x, f_send_z, f_recv_z,
        send_sems, recv_sems, arg_sems,
    ) = refs[28:]
    (
        species, send_list, vectors, neighbour, center,
        embed, w_src, w_rad0, w_rad1, w_inv, w_out, w_gate, w_energy,
    ) = held
    atoms = species.shape[1]
    edges = center.shape[1]
    sends = send_list.shape[1]
    width = w_out.shape[1]
    chan = w_gate.shape[1]
    rows_y = 9 * sends
    rest = REST * sends
    corner = 9 * sends - rest
    early = atoms + 27 * sends - 2 * corner
    unit = 8
    blocks = atoms // sends + 27

    parity = lax.rem(lax.axis_index("gy"), 2)
    plane_by = {OTHER: 2 * parity - 1, OWN: 0, MATE: 1 - 2 * parity}

    def device(plane=OWN, **steps):
        result = {}
        if plane != OWN:
            steps["gy"] = plane_by[plane]
        for axis, by in steps.items():
            size = lax.axis_size(axis)
            result[axis] = lax.rem(lax.axis_index(axis) + size + by, size)
        return result

    barrier = pltpu.get_barrier_semaphore()
    greeted = [device(gz=by) for by in (1, -1)] + [device(gx=by) for by in (1, -1)]
    greeted += [device(OTHER), device(MATE)] + [device(OTHER, gx=by) for by in (1, -1)]
    for other in greeted:
        pl.semaphore_signal(barrier, inc=1, device_id=other, device_id_type=MESH)
    loads = [
        pltpu.make_async_copy(source, target, arg_sems.at[i])
        for i, (source, target) in enumerate(zip(args, held))
    ]
    for load in loads:
        load.start()

    next_sem = [0]
    started = []

    def send(source, target, other):
        slot = next_sem[0]
        next_sem[0] = slot + 1
        copy = pltpu.make_async_remote_copy(
            src_ref=source, dst_ref=target, send_sem=send_sems.at[slot], recv_sem=recv_sems.at[slot],
            device_id=other, device_id_type=MESH,
        )
        copy.start()
        started.append(copy)
        return copy

    def settle(count):
        for copy in started[:count]:
            copy.wait_send()
        del started[:count]

    def spread(ref, size, pieces, between):
        def at(b, a, c, piece):
            return ref.at[pl.ds(position(b, a, c) * size + piece * (size // pieces), size // pieces)]

        def arrived(copies):
            for copy in copies:
                copy.wait_recv()

        def along(c, piece):
            return [send(at(OWN, 1, c, piece), at(OWN, a, c, piece), device(gx=1 - a)) for a in (0, 2)]

        def across(a, c, piece):
            return [send(at(OWN, a, c, piece), at(b, a, c, piece), device(b)) for b in (OTHER, MATE)]

        every = range(pieces)
        in_z = [
            [send(at(OWN, 1, 1, piece), at(OWN, 1, c, piece), device(gz=1 - c)) for c in (0, 2)] for piece in every
        ]
        in_x = [along(1, piece) for piece in every]
        near, last = [], []
        for piece in every:
            near += across(1, 1, piece)
        between[0]()
        for piece in every:
            arrived(in_x[piece])
            near += across(0, 1, piece) + across(2, 1, piece)
        in_x = []
        for piece in every:
            arrived(in_z[piece])
            in_x.append(along(0, piece) + along(2, piece))
            near += across(1, 0, piece) + across(1, 2, piece)
        between[1]()
        for piece in every:
            arrived(in_x[piece])
            for c in (0, 2):
                last += across(0, c, piece) + across(2, c, piece)
        arrived(near)
        between[2]()
        arrived(last)

    loads[0].wait()
    loads[1].wait()
    lane = lax.broadcasted_iota(jnp.int32, (atoms, atoms), 0)
    kind_t = jnp.where(lane == species[...], 1.0, 0.0).astype(BF16)
    lend_t = jnp.where(
        lax.broadcasted_iota(jnp.int32, (atoms, sends), 0) == send_list[...], 1.0, 0.0
    ).astype(BF16)
    lend_wide = mm_nt(eye(128, sends), lend_t).astype(BF16)
    lend = lend_wide[:sends]
    species_rows = jnp.broadcast_to(species[...].astype(F32), (unit, atoms))
    kinds[pl.ds(position(OWN, 1, 1) * unit, unit), :] = mm_nt(species_rows.astype(BF16), lend_wide)
    pl.semaphore_wait(barrier, len(greeted))


    def geometry():
        for load in loads[2:5]:
            load.wait()
        live = lax.broadcasted_iota(jnp.int32, (1, edges), 1) < edge_count[0, 0, 0]
        x = jnp.where(live, vectors[0], 1.0)
        y = jnp.where(live, vectors[1], 1.0)
        z = jnp.where(live, vectors[2], 1.0)
        square = x * x + y * y + z * z
        inverse = lax.rsqrt(square)
        distance = square * inverse
        ux, uy, uz = x * inverse, y * inverse, z * inverse
        for row, value in enumerate((ux, uy, uz, inverse)):
            geo[pl.ds(row, 1), :] = value
        for row, value in enumerate((
            ux, uy, uz, root * ux * uy, root * uy * uz, 0.5 * (3.0 * uz * uz - 1.0), root * ux * uz,
            0.5 * root * (ux * ux - uy * uy),
        )):
            harm[pl.ds(row, 1), :] = value
        sine, cosine = sin_cos(distance * (math.pi / CUTOFF))
        ratio = distance * (1.0 / CUTOFF)
        rest = 1.0 - ratio * ratio
        scale = rest * rest * inverse
        dscale = -(4.0 / CUTOFF) * rest * ratio * inverse - scale * inverse
        sin_k, cos_k = sine, cosine
        basis[...] = jnp.zeros_like(basis)
        for k in range(1, RADIAL + 1):
            basis[pl.ds(k - 1, 1), :] = sin_k * scale
            dbas[pl.ds(k - 1, 1), :] = (k * math.pi / CUTOFF) * cos_k * scale + sin_k * dscale
            sin_k, cos_k = sin_k * cosine + cos_k * sine, cos_k * cosine - sin_k * sine

        place = jnp.where(live, neighbour[...], -1)
        middle = jnp.where(live, center[...], -1)
        block = lax.shift_right_arithmetic(place, sends.bit_length() - 1)
        slot = lax.bitwise_and(place, sends - 1)
        planes = {plane: 1 + by for plane, by in plane_by.items()}
        order = {
            position(b, a, c): (a * 3 + planes[b]) * 3 + c for a in range(3) for b in planes for c in range(3)
        }
        rows = lax.broadcasted_iota(jnp.int32, (32, 1), 0)
        block_ids = rows
        for i in range(27):
            block_ids = jnp.where(rows == atoms // sends + i, atoms // sends + order[i], block_ids)
        block_of[...] = jnp.where(block_ids == block, 1.0, 0.0).astype(BF16)
        rows = lax.broadcasted_iota(jnp.int32, (atoms, edges), 0)
        slot_of[...] = jnp.where(rows == slot, 1.0, 0.0).astype(BF16)
        onehot_c[...] = jnp.where(rows == middle, 1.0, 0.0).astype(BF16)
        onehot[pl.ds(0, atoms), :] = jnp.where(rows == place, 1.0, 0.0).astype(BF16)
        rows = lax.broadcasted_iota(jnp.int32, (sends, edges), 0)
        for i in range(27):
            onehot[pl.ds(atoms + i * sends, sends), :] = jnp.where(
                rows == place - (atoms + order[i] * sends), 1.0, 0.0
            ).astype(BF16)

    def sweep(tile, work):
        if tile < 0:
            for i in range(edges // -tile):
                work(pl.ds(i * -tile, -tile))
        elif tile == edges:
            work(pl.ds(0, edges))
        else:
            lax.fori_loop(
                0, edges // tile, lambda i, carry: (work(pl.ds(pl.multiple_of(i * tile, tile), tile)), carry)[1], 0
            )

    def radial():
        for load in loads[5:]:
            load.wait()
        rad0_t = jnp.concatenate(
            [
                turned(
                    jnp.concatenate(
                        [w_rad0[l].astype(F32), jnp.zeros((8, w_rad0.shape[2]), F32)], axis=0
                    ).astype(BF16)
                ).astype(F32)
                for l in range(2)
            ],
            axis=0,
        ).astype(BF16)
        rad1_t1 = turned(w_rad1[0][:, : width + chan])
        rad1_t2 = turned(w_rad1[1][:, :width])

        def prepare(span):
            pre = mm(rad0_t, basis[:, span].astype(BF16))
            sig = jax.nn.sigmoid(pre)
            slope[:, span] = sig * (1.0 + pre * (1.0 - sig))
            hidden = (pre * sig).astype(BF16)
            rad1[:, span] = mm(rad1_t1, hidden[:hid])
            rad2[:, span] = mm(rad1_t2, hidden[hid:])

        sweep(edges, prepare)

        src2[...] = turned(w_src[1][:width])
        gate_w[...] = turned(w_gate[0])
        inv_t[...] = turned(w_inv[1])
        for layer in range(2):
            out_t[layer] = turned(w_out[layer])
        embed_rows = jnp.concatenate([embed[...], jnp.zeros((16 - embed.shape[0], width), F32)], axis=0)
        embed_t = turned(embed_rows.astype(BF16))
        kind_proj[...] = mm(w_src[0], embed_t).astype(BF16)
        start[...] = mm(embed_t, kind_t[:16, :])
        readout[...] = jnp.broadcast_to(w_energy[...], (width, width)).T

    root = math.sqrt(3.0)
    hid = w_rad0.shape[2]
    spread(kinds, unit, 1, (geometry, radial, lambda: None))
    number = species_rows[:1]
    kind_rows = [number] + [pltpu.roll(number, atoms - j * sends, 1) for j in range(1, atoms // sends)]
    kind_rows += [kinds[pl.ds(i * unit, 1), :] for i in range(27)]
    kind_rows += [jnp.zeros((1, atoms), F32)] * (32 - blocks)
    kind_table = mm_nt(eye(sends, atoms), jnp.concatenate(kind_rows, axis=0).astype(BF16)).astype(BF16)

    def layer_one(span):
        kind = sum_rows(mm(kind_table, block_of[:, span]) * slot_of[pl.ds(0, sends), span].astype(F32))
        kind_ids = lax.broadcasted_iota(jnp.int32, (16, kind.shape[1]), 0).astype(F32)
        proj = mm(kind_proj[...], jnp.where(kind_ids == kind, 1.0, 0.0).astype(BF16))
        proj1[:, span] = proj
        lead_s = proj[:width] * rad1[pl.ds(0, width), span]
        lead_t = proj[width:] * rad1[pl.ds(width, chan), span]
        parts = [lead_s.astype(BF16)]
        for m in range(8):
            parts.append((lead_t * harm[pl.ds(m, 1), span]).astype(BF16))
        agg[...] = mm_nt(jnp.concatenate(parts, axis=0), onehot_c[:, span])

    sweep(edges, layer_one)
    gathered = 0.25 * agg[...]
    gathered_t = gathered[width:]
    rounded = gathered[:width].astype(BF16)
    pre1 = mm(out_t[0], rounded)
    sig1 = jax.nn.sigmoid(pre1)
    gate = jax.nn.sigmoid(mm(w_gate[0], rounded))
    scalars = (start[...] + pre1 * sig1).astype(BF16)
    gates = jnp.concatenate([gate] * 8, axis=0)
    tensors = (gathered_t * gates).astype(BF16)
    proj2 = mm(w_src[1], scalars).astype(BF16)
    local = jnp.concatenate([proj2[:width], tensors], axis=0)
    halo[pl.ds(position(OWN, 1, 1) * sends, sends), :] = mm_nt(lend, local).astype(BF16)
    table[:, pl.ds(0, atoms)] = local
    earlier = len(started)

    def lookup(span):
        picked[:, span] = mm(table[...], onehot[pl.ds(0, early), span]).astype(BF16)

    def early_rows():
        table[:, pl.ds(atoms, early - atoms)] = halo[pl.ds(0, early - atoms), :].T
        sweep(edges, lookup)

    spread(halo, sends, 1, (lambda: settle(earlier), lambda: None, early_rows))
    last_table[...] = halo[pl.ds(early - atoms, 2 * corner), :].T

    def layer_two(span):
        rows = picked[:, span].astype(F32) + mm(last_table[...], onehot[pl.ds(early, 2 * corner), span])
        picked[:, span] = rows.astype(BF16)
        inner = jnp.zeros((chan, span.size), F32)
        for m in range(8):
            inner += rows[width + m * chan : width + (m + 1) * chan] * harm[pl.ds(m, 1), span]
        message = rows[:width] * rad2[:, span] + mm(inv_t[...], inner.astype(BF16))
        agg2[...] = mm_nt(message.astype(BF16), onehot_c[:, span])

    sweep(edges, layer_two)
    rounded = (0.25 * agg2[...]).astype(BF16)
    pre2 = mm(out_t[1], rounded)
    sig2 = jax.nn.sigmoid(pre2)
    mask = jnp.where(
        lax.broadcasted_iota(jnp.int32, (1, atoms), 1) < atom_count[0, 0, 0], 1.0, 0.0
    )
    energies[...] = mask * sum_rows((scalars.astype(F32) + pre2 * sig2) * readout[...])

    d_new = readout[...] * mask
    d_pre = (d_new * sig2 * (1.0 + pre2 * (1.0 - sig2))).astype(BF16)
    d_agg = (0.25 * mm(w_out[1], d_pre).astype(BF16).astype(F32)).astype(BF16)

    def back_two(span):
        d_msg = mm(d_agg, onehot_c[:, span])
        dmsg[pl.ds(0, width), span] = (d_msg * rad2[:, span]).astype(BF16)
        d_inv = mm(w_inv[1], d_msg.astype(BF16))
        for m in range(8):
            dmsg[pl.ds(width + m * chan, chan), span] = (d_inv * harm[pl.ds(m, 1), span]).astype(BF16)

    sweep(edges, back_two)
    earlier = len(started)

    def scattered(plane, corners):
        first = atoms + position(plane, *PLANE[REST if corners else 0][::-1]) * sends
        return mm_nt(onehot[pl.ds(first, corner if corners else rest), :], dmsg[...])

    def rows_of(c, a):
        return pl.ds(PLANE.index((c, a)) * sends, sends)

    halves = {True: pl.ds(rest, corner), False: pl.ds(0, rest)}
    back_o, back_m, back_x, plane = {}, {}, {}, {}

    def over(c, a):
        rows = rows_of(c, a)
        back_o[c, a] = send(back_send_o.at[rows], back_recv_o.at[rows], device(OTHER, gx=a - 1))

    def to_mate(corners):
        rows = halves[corners]
        back_send_m[rows] = scattered(MATE, corners).astype(BF16)
        back_m[corners] = send(back_send_m.at[rows], back_recv_m.at[rows], device(MATE))

    def own_rows(corners):
        sums = scattered(OWN, corners)
        back_m[corners].wait_recv()
        sums = sums + back_recv_m[halves[corners]].astype(F32)
        cells = PLANE[REST:] if corners else PLANE[:REST]
        for i, cell in enumerate(cells):
            plane[cell] = sums[i * sends : (i + 1) * sends]
        for c, a in cells:
            if a != 1:
                rows = rows_of(c, a)
                back_send_x[rows] = plane[c, a].astype(BF16)
                back_x[c, a] = send(back_send_x.at[rows], back_recv_x.at[rows], device(gx=a - 1))

    back_send_o[halves[True]] = scattered(OTHER, True).astype(BF16)
    for cell in PLANE[REST:]:
        over(*cell)
    to_mate(True)
    own_rows(True)
    back_send_o[halves[False]] = scattered(OTHER, False).astype(BF16)
    for cell in PLANE[:REST]:
        over(*cell)
    to_mate(False)
    own_rows(False)
    d_local = mm_nt(dmsg[...], onehot[pl.ds(0, atoms), :])

    def edge_two(span):
        d_msg = mm(d_agg, onehot_c[:, span])
        d_inv = mm(w_inv[1], d_msg.astype(BF16))
        for m in range(8):
            grad_y[pl.ds(m, 1), span] = sum_rows(
                d_inv * picked[pl.ds(width + m * chan, chan), span].astype(F32)
            )
        d_rad = (d_msg * picked[pl.ds(0, width), span].astype(F32)).astype(BF16)
        d_hid = mm(w_rad1[1][:, :width], d_rad) * slope[pl.ds(hid, hid), span]
        d_bas = mm(w_rad0[1], d_hid.astype(BF16))
        grad_d[:, span] = sum_rows(d_bas * dbas[:, span])

    sweep(edges, edge_two)

    settle(earlier)

    def gathered(c):
        total = plane[c, 1]
        for a in range(3):
            back_o[c, a].wait_recv()
            total = total + back_recv_o[rows_of(c, a)].astype(F32)
        for a in (0, 2):
            back_x[c, a].wait_recv()
            total = total + back_recv_x[rows_of(c, a)].astype(F32)
        return total

    back_z = []
    for slot, c in ((0, 0), (1, 2)):
        back_send_z[slot] = gathered(c).astype(BF16)
        back_z.append(send(back_send_z.at[slot], back_recv_z.at[slot], device(gz=c - 1)))
    back = gathered(1)
    settle(len(started) - 2)
    for copy in back_z:
        copy.wait_recv()
    back = back + back_recv_z[0].astype(F32) + back_recv_z[1].astype(F32)
    owned = d_local + mm(back.T.astype(BF16), lend)

    d_scalars = (d_new + mm(src2[...], owned[:width].astype(BF16))).astype(BF16).astype(F32)
    d_tensors = owned[width:].astype(BF16).astype(F32)
    d_pre = (d_scalars * sig1 * (1.0 + pre1 * (1.0 - sig1))).astype(BF16)
    product = d_tensors * gathered_t
    d_gate = jnp.zeros((chan, atoms), F32)
    for m in range(8):
        d_gate += product[m * chan : (m + 1) * chan]
    d_gate = (d_gate * gate * (1.0 - gate)).astype(BF16)
    d_scalar_agg = (mm(w_out[0], d_pre) + mm(gate_w[...], d_gate)).astype(BF16).astype(F32)
    d_agg1 = (0.25 * jnp.concatenate([d_scalar_agg, d_tensors * gates], axis=0)).astype(BF16)

    def edge_one(span):
        d_msg = mm(d_agg1, onehot_c[:, span])
        proj = proj1[:, span]
        lead_t = proj[width:] * rad1[pl.ds(width, chan), span]
        inner = jnp.zeros((chan, span.size), F32)
        gy = []
        for m in range(8):
            d_part = d_msg[width + m * chan : width + (m + 1) * chan]
            inner += d_part * harm[pl.ds(m, 1), span]
            gy.append(grad_y[pl.ds(m, 1), span] + sum_rows(d_part * lead_t))
        d_rad = jnp.concatenate([d_msg[:width], inner], axis=0) * proj
        d_hid = mm(w_rad1[0][:, : width + chan], d_rad.astype(BF16)) * slope[pl.ds(0, hid), span]
        d_bas = mm(w_rad0[0], d_hid.astype(BF16))
        gd = grad_d[:, span] + sum_rows(d_bas * dbas[:, span])
        ax, ay, az = geo[0:1, span], geo[1:2, span], geo[2:3, span]
        gux = gy[0] + root * (ay * gy[3] + az * gy[6] + ax * gy[7])
        guy = gy[1] + root * (ax * gy[3] + az * gy[4] - ay * gy[7])
        guz = gy[2] + root * (ay * gy[4] + ax * gy[6]) + 3.0 * az * gy[5]
        radial = gd - geo[3:4, span] * (ax * gux + ay * guy + az * guz)
        pull[pl.ds(0, 1), span] = geo[3:4, span] * gux + ax * radial
        pull[pl.ds(1, 1), span] = geo[3:4, span] * guy + ay * radial
        pull[pl.ds(2, 1), span] = geo[3:4, span] * guz + az * radial

    pull[...] = jnp.zeros_like(pull)
    sweep(edges, edge_one)

    pulls = pull[...]
    high = pulls.astype(BF16).astype(F32)
    pulls = high + pltpu.roll(pulls - high, 3, 0)
    for i in range(0, 32, 2):
        f_rows[pl.ds(i * unit, 2 * unit), :] = jnp.concatenate(
            [pulls * block_of[pl.ds(j, 1), :].astype(F32) for j in (i, i + 1)], axis=0
        ).astype(BF16)
    f_all[...] = mm_nt(f_rows[...], slot_of[...])
    first = (atoms // sends) * unit

    def cell(b, a, c):
        return f_all[pl.ds(first + position(b, a, c) * unit, unit), :]

    for a in range(3):
        f_send_o[a] = jnp.concatenate([cell(OTHER, a, c) for c in range(3)], axis=0)
    f_send_m[...] = jnp.concatenate([cell(MATE, a, c) for a in range(3) for c in range(3)], axis=0)
    f_m = send(f_send_m, f_recv_m, device(MATE))
    f_o = [send(f_send_o.at[a], f_recv_o.at[a], device(OTHER, gx=a - 1)) for a in (0, 2, 1)]
    lines = jnp.concatenate([cell(OWN, a, c) for a in range(3) for c in range(3)], axis=0)
    f_m.wait_recv()
    lines = lines + f_recv_m[...]
    f_x = []
    for slot, a in ((0, 0), (1, 2)):
        f_send_x[slot] = lines[3 * a * unit : 3 * (a + 1) * unit]
        f_x.append(send(f_send_x.at[slot], f_recv_x.at[slot], device(gx=a - 1)))
    total = mm_nt(pulls.astype(BF16), onehot_c[...])
    for j in range(atoms // sends):
        block = f_all[pl.ds(j * unit, unit), :]
        total = total - (block if j == 0 else pltpu.roll(block, j * sends, 1))
    settle(len(started) - 2)
    for copy in f_x + f_o:
        copy.wait_recv()
    lines = lines[3 * unit : 6 * unit] + f_recv_x[0] + f_recv_x[1] + f_recv_o[0] + f_recv_o[1] + f_recv_o[2]
    f_z = []
    for slot, c in ((0, 0), (1, 2)):
        f_send_z[slot] = lines[c * unit : (c + 1) * unit]
        f_z.append(send(f_send_z.at[slot], f_recv_z.at[slot], device(gz=c - 1)))
    for copy in f_z:
        copy.wait_recv()
    lines = lines[unit : 2 * unit] + f_recv_z[0] + f_recv_z[1]
    total = total - joined(mm(split(lines), lend_wide))
    for row in range(3):
        forces[row] = total[row : row + 1] + total[row + 3 : row + 4]
    settle(len(started))


def per_device(
    species, atom_count, send_list, edge_count, edge_center, edge_neighbour, edge_vectors,
    embed, w_src, w_rad0, w_rad1, w_inv, w_out, w_gate, w_energy,
):
    atoms = species.shape[-1]
    edges = edge_center.shape[-1]
    sends = send_list.shape[-1]
    width = w_out.shape[1]
    chan = w_gate.shape[2]
    hid = w_rad0.shape[2]
    cols = width + 8 * chan
    ghosts = 27 * sends
    unit = 8
    early = atoms + (9 + 2 * REST) * sends
    vmem = pl.BlockSpec(memory_space=pltpu.VMEM)
    smem = pl.BlockSpec(memory_space=pltpu.SMEM)
    hbm = pl.BlockSpec(memory_space=pltpu.HBM)
    copies = 26 + 26 * 1 + 19 + 8
    operands = (
        species.reshape(1, atoms), send_list.reshape(1, sends), edge_vectors.reshape(3, 1, edges),
        edge_neighbour.reshape(1, edges), edge_center.reshape(1, edges),
        embed, jnp.swapaxes(w_src, 1, 2), w_rad0, w_rad1, w_inv, w_out, jnp.swapaxes(w_gate, 1, 2),
        w_energy.reshape(1, width),
    )
    energies, forces = pl.pallas_call(
        body,
        out_shape=(
            jax.ShapeDtypeStruct((1, atoms), F32),
            jax.ShapeDtypeStruct((3, 1, atoms), F32),
        ),
        in_specs=[smem, smem] + [hbm] * len(operands),
        out_specs=(vmem, vmem),
        scratch_shapes=[pltpu.VMEM(operand.shape, operand.dtype) for operand in operands] + [
            pltpu.VMEM((atoms + ghosts, edges), BF16),
            pltpu.VMEM((atoms, edges), BF16),
            pltpu.VMEM((32, edges), BF16),
            pltpu.VMEM((atoms, edges), BF16),
            pltpu.VMEM((27 * unit, atoms), F32),
            pltpu.VMEM((ghosts, cols), BF16),
            pltpu.VMEM((cols, early), BF16),
            pltpu.VMEM((cols, ghosts + atoms - early), BF16),
            pltpu.VMEM((cols, edges), BF16),
            pltpu.VMEM((cols, edges), BF16),
            pltpu.VMEM((8, edges), F32),
            pltpu.VMEM((8, edges), F32),
            pltpu.VMEM((8, edges), F32),
            pltpu.VMEM((16, edges), F32),
            pltpu.VMEM((2 * hid, edges), F32),
            pltpu.VMEM((width + chan, edges), F32),
            pltpu.VMEM((width, edges), F32),
            pltpu.VMEM((width + chan, edges), F32),
            pltpu.VMEM((width, width), BF16),
            pltpu.VMEM((width, chan), BF16),
            pltpu.VMEM((width, chan), BF16),
            pltpu.VMEM((2, width, width), BF16),
            pltpu.VMEM((width + chan, 16), BF16),
            pltpu.VMEM((width, atoms), F32),
            pltpu.VMEM((width, width), F32),
            pltpu.VMEM((32 * unit, edges), BF16),
            pltpu.VMEM((cols, atoms), F32),
            pltpu.VMEM((width, atoms), F32),
            pltpu.VMEM((8, edges), F32),
            pltpu.VMEM((1, edges), F32),
            pltpu.VMEM((8, edges), F32),
            pltpu.VMEM((9 * sends, cols), BF16),
            pltpu.VMEM((9 * sends, cols), BF16),
            pltpu.VMEM((9 * sends, cols), BF16),
            pltpu.VMEM((9 * sends, cols), BF16),
            pltpu.VMEM((9 * sends, cols), BF16),
            pltpu.VMEM((9 * sends, cols), BF16),
            pltpu.VMEM((2, sends, cols), BF16),
            pltpu.VMEM((2, sends, cols), BF16),
            pltpu.VMEM((32 * unit, 128), F32),
            pltpu.VMEM((3, 3 * unit, 128), F32),
            pltpu.VMEM((3, 3 * unit, 128), F32),
            pltpu.VMEM((9 * unit, 128), F32),
            pltpu.VMEM((9 * unit, 128), F32),
            pltpu.VMEM((2, 3 * unit, 128), F32),
            pltpu.VMEM((2, 3 * unit, 128), F32),
            pltpu.VMEM((2, unit, 128), F32),
            pltpu.VMEM((2, unit, 128), F32),
            pltpu.SemaphoreType.DMA((copies,)),
            pltpu.SemaphoreType.DMA((copies,)),
            pltpu.SemaphoreType.DMA((len(operands),)),
        ],
        compiler_params=pltpu.CompilerParams(
            collective_id=0, has_side_effects=True, vmem_limit_bytes=56 * 1024 * 1024
        ),
    )(atom_count, edge_count, *operands)
    return energies.reshape(species.shape), forces.reshape(edge_vectors.shape[:3] + (3, atoms))


def solution(mesh):
    shard = P("gx", "gy", "gz", None)
    count = P("gx", "gy", "gz")
    wide = P("gx", "gy", "gz", None, None)
    return jax.shard_map(
        per_device,
        mesh=mesh,
        in_specs=(shard, count, shard, count, shard, shard, wide) + (P(),) * 8,
        out_specs=(shard, wide),
        check_vma=False,
    )
```

```python
import functools
import math

import jax
import jax.numpy as jnp
from jax import lax
from jax.experimental import pallas as pl
from jax.experimental.pallas import tpu as pltpu
from jax.sharding import PartitionSpec as P

RADIAL = 8
CUTOFF = 5.0
PLANE = ((1, 0), (1, 1), (1, 2), (0, 1), (2, 1), (0, 0), (0, 2), (2, 0), (2, 2))
REST = 5
OTHER, OWN, MATE = 0, 1, 2


def position(b, a, c):
    index = PLANE.index((c, a))
    if b == OWN:
        return index
    if index < REST:
        return 9 + (b // 2) * REST + index
    return 9 + 2 * REST + (b // 2) * (9 - REST) + index - REST


MESH = pl.DeviceIdType.MESH
BF16 = jnp.bfloat16
F32 = jnp.float32


def mm(left, right):
    return lax.dot_general(left, right, (((1,), (0,)), ((), ())), preferred_element_type=F32)


def mm_nt(left, right):
    return lax.dot_general(left, right, (((1,), (1,)), ((), ())), preferred_element_type=F32)


def eye(rows, cols):
    first = lax.broadcasted_iota(jnp.int32, (rows, cols), 0)
    second = lax.broadcasted_iota(jnp.int32, (rows, cols), 1)
    return jnp.where(first == second, 1.0, 0.0).astype(BF16)


def turned(array):
    return mm_nt(eye(array.shape[1], array.shape[1]), array).astype(BF16)


def split(array):
    high = array.astype(BF16).astype(F32)
    return jnp.concatenate([high, array - high], axis=0).astype(BF16)


def joined(array):
    half = array.shape[0] // 2
    return array[:half] + array[half:]


def sum_rows(array):
    return jnp.sum(array, axis=0, keepdims=True)


def sin_cos(angle):
    y = angle - (math.pi / 2)
    y2 = y * y
    sin_y = jnp.full_like(y, -1.0 / math.factorial(11))
    for power in (9, 7, 5, 3, 1):
        sin_y = sin_y * y2 + ((-1.0) ** (power // 2)) / math.factorial(power)
    cos_y = jnp.full_like(y, 1.0 / math.factorial(12))
    for power in (10, 8, 6, 4, 2, 0):
        cos_y = cos_y * y2 + ((-1.0) ** (power // 2)) / math.factorial(power)
    return cos_y, -(sin_y * y)


def body(
    atom_count, edge_count, *refs
):
    args, (energies, forces), held = refs[:13], refs[13:15], refs[15:28]
    (
        onehot, onehot_c, block_of, slot_of, kinds, halo, table, last_table, picked, dmsg,
        geo, harm, dbas, basis, slope, rad1, rad2, proj1, src2, gate_w, inv_t, out_t, kind_proj, start, readout, f_rows, agg, agg2, grad_y, grad_d, pull,
        back_send_o, back_recv_o, back_send_m, back_recv_m, back_send_x, back_recv_x, back_send_z, back_recv_z,
        f_all, f_send_o, f_recv_o, f_send_m, f_recv_m, f_send_x, f_recv_x, f_send_z, f_recv_z,
        send_sems, recv_sems, arg_sems,
    ) = refs[28:]
    (
        species, send_list, vectors, neighbour, center,
        embed, w_src, w_rad0, w_rad1, w_inv, w_out, w_gate, w_energy,
    ) = held
    atoms = species.shape[1]
    edges = center.shape[1]
    sends = send_list.shape[1]
    width = w_out.shape[1]
    chan = w_gate.shape[1]
    rows_y = 9 * sends
    rest = REST * sends
    corner = 9 * sends - rest
    early = atoms + 27 * sends - 2 * corner
    unit = 8
    blocks = atoms // sends + 27

    parity = lax.rem(lax.axis_index("gy"), 2)
    plane_by = {OTHER: 2 * parity - 1, OWN: 0, MATE: 1 - 2 * parity}

    def device(plane=OWN, **steps):
        result = {}
        if plane != OWN:
            steps["gy"] = plane_by[plane]
        for axis, by in steps.items():
            size = lax.axis_size(axis)
            result[axis] = lax.rem(lax.axis_index(axis) + size + by, size)
        return result

    loads = [
        pltpu.make_async_copy(source, target, arg_sems.at[i])
        for i, (source, target) in enumerate(zip(args, held))
    ]
    for load in loads[:2]:
        load.start()

    barrier = pltpu.get_barrier_semaphore()
    greeted = [device(gz=by) for by in (1, -1)] + [device(gx=by) for by in (1, -1)]
    greeted += [device(OTHER), device(MATE)] + [device(OTHER, gx=by) for by in (1, -1)]
    for other in greeted:
        pl.semaphore_signal(barrier, inc=1, device_id=other, device_id_type=MESH)
    for load in loads[2:5]:
        load.start()

    next_sem = [0]
    started = []

    def send(source, target, other):
        slot = next_sem[0]
        next_sem[0] = slot + 1
        copy = pltpu.make_async_remote_copy(
            src_ref=source, dst_ref=target, send_sem=send_sems.at[slot], recv_sem=recv_sems.at[slot],
            device_id=other, device_id_type=MESH,
        )
        copy.start()
        started.append(copy)
        return copy

    def settle(count):
        for copy in started[:count]:
            copy.wait_send()
        del started[:count]

    def spread(ref, size, pieces, between, straight=False):
        near, last = [], []

        def at(b, a, c, piece):
            return ref.at[pl.ds(position(b, a, c) * size + piece * (size // pieces), size // pieces)]

        def arrived(copies):
            for copy in copies:
                copy.wait_recv()

        def along(c, piece):
            copies = [send(at(OWN, 1, c, piece), at(OWN, a, c, piece), device(gx=1 - a)) for a in (0, 2)]
            for a in (0, 2) if straight else ():
                last.append(send(at(OWN, 1, c, piece), at(OTHER, a, c, piece), device(OTHER, gx=1 - a)))
            return copies

        def across(a, c, piece):
            planes = (MATE,) if straight and a != 1 else (OTHER, MATE)
            return [send(at(OWN, a, c, piece), at(b, a, c, piece), device(b)) for b in planes]

        every = range(pieces)
        in_z = [
            [send(at(OWN, 1, 1, piece), at(OWN, 1, c, piece), device(gz=1 - c)) for c in (0, 2)] for piece in every
        ]
        in_x = [along(1, piece) for piece in every]
        for piece in every:
            near += across(1, 1, piece)
        between[0]()
        for piece in every:
            arrived(in_x[piece])
            near += across(0, 1, piece) + across(2, 1, piece)
        in_x = []
        for piece in every:
            arrived(in_z[piece])
            in_x.append(along(0, piece) + along(2, piece))
            near += across(1, 0, piece) + across(1, 2, piece)
        between[1]()
        for piece in every:
            arrived(in_x[piece])
            for c in (0, 2):
                last += across(0, c, piece) + across(2, c, piece)
        arrived(near)
        between[2]()
        arrived(last)

    loads[0].wait()
    loads[1].wait()
    lane = lax.broadcasted_iota(jnp.int32, (atoms, atoms), 0)
    kind_t = jnp.where(lane == species[...], 1.0, 0.0).astype(BF16)
    lend_t = jnp.where(
        lax.broadcasted_iota(jnp.int32, (atoms, sends), 0) == send_list[...], 1.0, 0.0
    ).astype(BF16)
    lend_wide = mm_nt(eye(128, sends), lend_t).astype(BF16)
    lend = lend_wide[:sends]
    species_rows = jnp.broadcast_to(species[...].astype(F32), (unit, atoms))
    kinds[pl.ds(position(OWN, 1, 1) * unit, unit), :] = mm_nt(species_rows.astype(BF16), lend_wide)
    pl.semaphore_wait(barrier, len(greeted))


    def geometry():
        for load in loads[5:]:
            load.start()
        for load in loads[2:5]:
            load.wait()
        live = lax.broadcasted_iota(jnp.int32, (1, edges), 1) < edge_count[0, 0, 0]
        x = jnp.where(live, vectors[0], 1.0)
        y = jnp.where(live, vectors[1], 1.0)
        z = jnp.where(live, vectors[2], 1.0)
        square = x * x + y * y + z * z
        inverse = lax.rsqrt(square)
        distance = square * inverse
        ux, uy, uz = x * inverse, y * inverse, z * inverse
        for row, value in enumerate((ux, uy, uz, inverse)):
            geo[pl.ds(row, 1), :] = value
        for row, value in enumerate((
            ux, uy, uz, root * ux * uy, root * uy * uz, 0.5 * (3.0 * uz * uz - 1.0), root * ux * uz,
            0.5 * root * (ux * ux - uy * uy),
        )):
            harm[pl.ds(row, 1), :] = value
        sine, cosine = sin_cos(distance * (math.pi / CUTOFF))
        ratio = distance * (1.0 / CUTOFF)
        rest = 1.0 - ratio * ratio
        scale = rest * rest * inverse
        dscale = -(4.0 / CUTOFF) * rest * ratio * inverse - scale * inverse
        sin_k, cos_k = sine, cosine
        basis[...] = jnp.zeros_like(basis)
        for k in range(1, RADIAL + 1):
            basis[pl.ds(k - 1, 1), :] = sin_k * scale
            dbas[pl.ds(k - 1, 1), :] = (k * math.pi / CUTOFF) * cos_k * scale + sin_k * dscale
            sin_k, cos_k = sin_k * cosine + cos_k * sine, cos_k * cosine - sin_k * sine

        place = jnp.where(live, neighbour[...], -1)
        middle = jnp.where(live, center[...], -1)
        block = lax.shift_right_arithmetic(place, sends.bit_length() - 1)
        slot = lax.bitwise_and(place, sends - 1)
        planes = {plane: 1 + by for plane, by in plane_by.items()}
        order = {
            position(b, a, c): (a * 3 + planes[b]) * 3 + c for a in range(3) for b in planes for c in range(3)
        }
        rows = lax.broadcasted_iota(jnp.int32, (32, 1), 0)
        block_ids = rows
        for i in range(27):
            block_ids = jnp.where(rows == atoms // sends + i, atoms // sends + order[i], block_ids)
        block_of[...] = jnp.where(block_ids == block, 1.0, 0.0).astype(BF16)
        rows = lax.broadcasted_iota(jnp.int32, (atoms, edges), 0)
        slot_of[...] = jnp.where(rows == slot, 1.0, 0.0).astype(BF16)
        onehot_c[...] = jnp.where(rows == middle, 1.0, 0.0).astype(BF16)
        onehot[pl.ds(0, atoms), :] = jnp.where(rows == place, 1.0, 0.0).astype(BF16)
        rows = lax.broadcasted_iota(jnp.int32, (sends, edges), 0)
        for i in range(27):
            onehot[pl.ds(atoms + i * sends, sends), :] = jnp.where(
                rows == place - (atoms + order[i] * sends), 1.0, 0.0
            ).astype(BF16)

    def sweep(tile, work):
        if tile < 0:
            for i in range(edges // -tile):
                work(pl.ds(i * -tile, -tile))
        elif tile == edges:
            work(pl.ds(0, edges))
        else:
            lax.fori_loop(
                0, edges // tile, lambda i, carry: (work(pl.ds(pl.multiple_of(i * tile, tile), tile)), carry)[1], 0
            )

    def radial():
        for load in loads[5:]:
            load.wait()
        rad0_t = jnp.concatenate(
            [
                turned(
                    jnp.concatenate(
                        [w_rad0[l].astype(F32), jnp.zeros((8, w_rad0.shape[2]), F32)], axis=0
                    ).astype(BF16)
                ).astype(F32)
                for l in range(2)
            ],
            axis=0,
        ).astype(BF16)
        rad1_t1 = turned(w_rad1[0][:, : width + chan])
        rad1_t2 = turned(w_rad1[1][:, :width])

        def prepare(span):
            pre = mm(rad0_t, basis[:, span].astype(BF16))
            sig = jax.nn.sigmoid(pre)
            slope[:, span] = sig * (1.0 + pre * (1.0 - sig))
            hidden = (pre * sig).astype(BF16)
            rad1[:, span] = mm(rad1_t1, hidden[:hid])
            rad2[:, span] = mm(rad1_t2, hidden[hid:])

        sweep(edges, prepare)

        src2[...] = turned(w_src[1][:width])
        gate_w[...] = turned(w_gate[0])
        inv_t[...] = turned(w_inv[1])
        for layer in range(2):
            out_t[layer] = turned(w_out[layer])
        embed_rows = jnp.concatenate([embed[...], jnp.zeros((16 - embed.shape[0], width), F32)], axis=0)
        embed_t = turned(embed_rows.astype(BF16))
        kind_proj[...] = mm(w_src[0], embed_t).astype(BF16)
        start[...] = mm(embed_t, kind_t[:16, :])
        readout[...] = jnp.broadcast_to(w_energy[...], (width, width)).T

    root = math.sqrt(3.0)
    hid = w_rad0.shape[2]
    spread(kinds, unit, 1, (geometry, radial, lambda: None), straight=True)
    number = species_rows[:1]
    kind_rows = [number] + [pltpu.roll(number, atoms - j * sends, 1) for j in range(1, atoms // sends)]
    kind_rows += [kinds[pl.ds(i * unit, 1), :] for i in range(27)]
    kind_rows += [jnp.zeros((1, atoms), F32)] * (32 - blocks)
    kind_table = mm_nt(eye(sends, atoms), jnp.concatenate(kind_rows, axis=0).astype(BF16)).astype(BF16)

    def layer_one(span):
        kind = sum_rows(mm(kind_table, block_of[:, span]) * slot_of[pl.ds(0, sends), span].astype(F32))
        kind_ids = lax.broadcasted_iota(jnp.int32, (16, kind.shape[1]), 0).astype(F32)
        proj = mm(kind_proj[...], jnp.where(kind_ids == kind, 1.0, 0.0).astype(BF16))
        proj1[:, span] = proj
        lead_s = proj[:width] * rad1[pl.ds(0, width), span]
        lead_t = proj[width:] * rad1[pl.ds(width, chan), span]
        parts = [lead_s.astype(BF16)]
        for m in range(8):
            parts.append((lead_t * harm[pl.ds(m, 1), span]).astype(BF16))
        agg[...] = mm_nt(jnp.concatenate(parts, axis=0), onehot_c[:, span])

    sweep(edges, layer_one)
    gathered = 0.25 * agg[...]
    gathered_t = gathered[width:]
    rounded = gathered[:width].astype(BF16)
    pre1 = mm(out_t[0], rounded)
    sig1 = jax.nn.sigmoid(pre1)
    gate = jax.nn.sigmoid(mm(w_gate[0], rounded))
    scalars = (start[...] + pre1 * sig1).astype(BF16)
    gates = jnp.concatenate([gate] * 8, axis=0)
    tensors = (gathered_t * gates).astype(BF16)
    proj2 = mm(w_src[1], scalars).astype(BF16)
    local = jnp.concatenate([proj2[:width], tensors], axis=0)
    halo[pl.ds(position(OWN, 1, 1) * sends, sends), :] = mm_nt(lend, local).astype(BF16)
    table[:, pl.ds(0, atoms)] = local
    earlier = len(started)

    def lookup(span):
        picked[:, span] = mm(table[...], onehot[pl.ds(0, early), span]).astype(BF16)

    def early_rows():
        table[:, pl.ds(atoms, early - atoms)] = halo[pl.ds(0, early - atoms), :].T
        sweep(edges, lookup)

    spread(halo, sends, 1, (lambda: settle(earlier), lambda: None, early_rows))
    last_table[...] = halo[pl.ds(early - atoms, 2 * corner), :].T

    def layer_two(span):
        rows = picked[:, span].astype(F32) + mm(last_table[...], onehot[pl.ds(early, 2 * corner), span])
        picked[:, span] = rows.astype(BF16)
        inner = jnp.zeros((chan, span.size), F32)
        for m in range(8):
            inner += rows[width + m * chan : width + (m + 1) * chan] * harm[pl.ds(m, 1), span]
        message = rows[:width] * rad2[:, span] + mm(inv_t[...], inner.astype(BF16))
        agg2[...] = mm_nt(message.astype(BF16), onehot_c[:, span])

    sweep(edges, layer_two)
    rounded = (0.25 * agg2[...]).astype(BF16)
    pre2 = mm(out_t[1], rounded)
    sig2 = jax.nn.sigmoid(pre2)
    mask = jnp.where(
        lax.broadcasted_iota(jnp.int32, (1, atoms), 1) < atom_count[0, 0, 0], 1.0, 0.0
    )
    energies[...] = mask * sum_rows((scalars.astype(F32) + pre2 * sig2) * readout[...])

    d_new = readout[...] * mask
    d_pre = (d_new * sig2 * (1.0 + pre2 * (1.0 - sig2))).astype(BF16)
    d_agg = (0.25 * mm(w_out[1], d_pre).astype(BF16).astype(F32)).astype(BF16)

    def back_two(span):
        d_msg = mm(d_agg, onehot_c[:, span])
        dmsg[pl.ds(0, width), span] = (d_msg * rad2[:, span]).astype(BF16)
        d_inv = mm(w_inv[1], d_msg.astype(BF16))
        for m in range(8):
            dmsg[pl.ds(width + m * chan, chan), span] = (d_inv * harm[pl.ds(m, 1), span]).astype(BF16)

    sweep(edges, back_two)
    earlier = len(started)

    def scattered(plane, corners):
        first = atoms + position(plane, *PLANE[REST if corners else 0][::-1]) * sends
        return mm_nt(onehot[pl.ds(first, corner if corners else rest), :], dmsg[...])

    def rows_of(c, a):
        return pl.ds(PLANE.index((c, a)) * sends, sends)

    halves = {True: pl.ds(rest, corner), False: pl.ds(0, rest)}
    back_o, back_m, back_x, plane = {}, {}, {}, {}

    def over(c, a):
        rows = rows_of(c, a)
        back_o[c, a] = send(back_send_o.at[rows], back_recv_o.at[rows], device(OTHER, gx=a - 1))

    def to_mate(corners):
        rows = halves[corners]
        back_send_m[rows] = scattered(MATE, corners).astype(BF16)
        back_m[corners] = send(back_send_m.at[rows], back_recv_m.at[rows], device(MATE))

    def own_rows(corners):
        sums = scattered(OWN, corners)
        back_m[corners].wait_recv()
        sums = sums + back_recv_m[halves[corners]].astype(F32)
        cells = PLANE[REST:] if corners else PLANE[:REST]
        for i, cell in enumerate(cells):
            plane[cell] = sums[i * sends : (i + 1) * sends]
        for c, a in cells:
            if a != 1:
                rows = rows_of(c, a)
                back_send_x[rows] = plane[c, a].astype(BF16)
                back_x[c, a] = send(back_send_x.at[rows], back_recv_x.at[rows], device(gx=a - 1))

    back_send_o[halves[True]] = scattered(OTHER, True).astype(BF16)
    for cell in PLANE[REST:]:
        over(*cell)
    to_mate(True)
    own_rows(True)
    back_send_o[halves[False]] = scattered(OTHER, False).astype(BF16)
    for cell in PLANE[:REST]:
        over(*cell)
    to_mate(False)
    own_rows(False)
    d_local = mm_nt(dmsg[...], onehot[pl.ds(0, atoms), :])

    def edge_two(span):
        d_msg = mm(d_agg, onehot_c[:, span])
        d_inv = mm(w_inv[1], d_msg.astype(BF16))
        for m in range(8):
            grad_y[pl.ds(m, 1), span] = sum_rows(
                d_inv * picked[pl.ds(width + m * chan, chan), span].astype(F32)
            )
        d_rad = (d_msg * picked[pl.ds(0, width), span].astype(F32)).astype(BF16)
        d_hid = mm(w_rad1[1][:, :width], d_rad) * slope[pl.ds(hid, hid), span]
        d_bas = mm(w_rad0[1], d_hid.astype(BF16))
        grad_d[:, span] = sum_rows(d_bas * dbas[:, span])

    sweep(edges, edge_two)

    settle(earlier)

    def gathered(c):
        total = plane[c, 1]
        for a in range(3):
            back_o[c, a].wait_recv()
            total = total + back_recv_o[rows_of(c, a)].astype(F32)
        for a in (0, 2):
            back_x[c, a].wait_recv()
            total = total + back_recv_x[rows_of(c, a)].astype(F32)
        return total

    back_z = []
    for slot, c in ((0, 0), (1, 2)):
        back_send_z[slot] = gathered(c).astype(BF16)
        back_z.append(send(back_send_z.at[slot], back_recv_z.at[slot], device(gz=c - 1)))
    back = gathered(1)
    settle(len(started) - 2)
    for copy in back_z:
        copy.wait_recv()
    back = back + back_recv_z[0].astype(F32) + back_recv_z[1].astype(F32)
    owned = d_local + mm(back.T.astype(BF16), lend)

    d_scalars = (d_new + mm(src2[...], owned[:width].astype(BF16))).astype(BF16).astype(F32)
    d_tensors = owned[width:].astype(BF16).astype(F32)
    d_pre = (d_scalars * sig1 * (1.0 + pre1 * (1.0 - sig1))).astype(BF16)
    product = d_tensors * gathered_t
    d_gate = jnp.zeros((chan, atoms), F32)
    for m in range(8):
        d_gate += product[m * chan : (m + 1) * chan]
    d_gate = (d_gate * gate * (1.0 - gate)).astype(BF16)
    d_scalar_agg = (mm(w_out[0], d_pre) + mm(gate_w[...], d_gate)).astype(BF16).astype(F32)
    d_agg1 = (0.25 * jnp.concatenate([d_scalar_agg, d_tensors * gates], axis=0)).astype(BF16)

    def edge_one(span):
        d_msg = mm(d_agg1, onehot_c[:, span])
        proj = proj1[:, span]
        lead_t = proj[width:] * rad1[pl.ds(width, chan), span]
        inner = jnp.zeros((chan, span.size), F32)
        gy = []
        for m in range(8):
            d_part = d_msg[width + m * chan : width + (m + 1) * chan]
            inner += d_part * harm[pl.ds(m, 1), span]
            gy.append(grad_y[pl.ds(m, 1), span] + sum_rows(d_part * lead_t))
        d_rad = jnp.concatenate([d_msg[:width], inner], axis=0) * proj
        d_hid = mm(w_rad1[0][:, : width + chan], d_rad.astype(BF16)) * slope[pl.ds(0, hid), span]
        d_bas = mm(w_rad0[0], d_hid.astype(BF16))
        gd = grad_d[:, span] + sum_rows(d_bas * dbas[:, span])
        ax, ay, az = geo[0:1, span], geo[1:2, span], geo[2:3, span]
        gux = gy[0] + root * (ay * gy[3] + az * gy[6] + ax * gy[7])
        guy = gy[1] + root * (ax * gy[3] + az * gy[4] - ay * gy[7])
        guz = gy[2] + root * (ay * gy[4] + ax * gy[6]) + 3.0 * az * gy[5]
        radial = gd - geo[3:4, span] * (ax * gux + ay * guy + az * guz)
        pull[pl.ds(0, 1), span] = geo[3:4, span] * gux + ax * radial
        pull[pl.ds(1, 1), span] = geo[3:4, span] * guy + ay * radial
        pull[pl.ds(2, 1), span] = geo[3:4, span] * guz + az * radial

    pull[...] = jnp.zeros_like(pull)
    sweep(edges, edge_one)

    pulls = pull[...]
    high = pulls.astype(BF16).astype(F32)
    pulls = high + pltpu.roll(pulls - high, 3, 0)
    for i in range(0, 32, 2):
        f_rows[pl.ds(i * unit, 2 * unit), :] = jnp.concatenate(
            [pulls * block_of[pl.ds(j, 1), :].astype(F32) for j in (i, i + 1)], axis=0
        ).astype(BF16)
    f_all[...] = mm_nt(f_rows[...], slot_of[...])
    first = (atoms // sends) * unit

    def cell(b, a, c):
        return f_all[pl.ds(first + position(b, a, c) * unit, unit), :]

    for a in range(3):
        f_send_o[a] = jnp.concatenate([cell(OTHER, a, c) for c in range(3)], axis=0)
    f_send_m[...] = jnp.concatenate([cell(MATE, a, c) for a in range(3) for c in range(3)], axis=0)
    f_m = send(f_send_m, f_recv_m, device(MATE))
    f_o = [send(f_send_o.at[a], f_recv_o.at[a], device(OTHER, gx=a - 1)) for a in (0, 2, 1)]
    lines = jnp.concatenate([cell(OWN, a, c) for a in range(3) for c in range(3)], axis=0)
    f_m.wait_recv()
    lines = lines + f_recv_m[...]
    f_x = []
    for slot, a in ((0, 0), (1, 2)):
        f_send_x[slot] = lines[3 * a * unit : 3 * (a + 1) * unit]
        f_x.append(send(f_send_x.at[slot], f_recv_x.at[slot], device(gx=a - 1)))
    total = mm_nt(pulls.astype(BF16), onehot_c[...])
    for j in range(atoms // sends):
        block = f_all[pl.ds(j * unit, unit), :]
        total = total - (block if j == 0 else pltpu.roll(block, j * sends, 1))
    settle(len(started) - 2)
    for copy in f_x + f_o:
        copy.wait_recv()
    lines = lines[3 * unit : 6 * unit] + f_recv_x[0] + f_recv_x[1] + f_recv_o[0] + f_recv_o[1] + f_recv_o[2]
    f_z = []
    for slot, c in ((0, 0), (1, 2)):
        f_send_z[slot] = lines[c * unit : (c + 1) * unit]
        f_z.append(send(f_send_z.at[slot], f_recv_z.at[slot], device(gz=c - 1)))
    for copy in f_z:
        copy.wait_recv()
    lines = lines[unit : 2 * unit] + f_recv_z[0] + f_recv_z[1]
    total = total - joined(mm(split(lines), lend_wide))
    for row in range(3):
        forces[row] = total[row : row + 1] + total[row + 3 : row + 4]
    settle(len(started))


def per_device(
    species, atom_count, send_list, edge_count, edge_center, edge_neighbour, edge_vectors,
    embed, w_src, w_rad0, w_rad1, w_inv, w_out, w_gate, w_energy,
):
    atoms = species.shape[-1]
    edges = edge_center.shape[-1]
    sends = send_list.shape[-1]
    width = w_out.shape[1]
    chan = w_gate.shape[2]
    hid = w_rad0.shape[2]
    cols = width + 8 * chan
    ghosts = 27 * sends
    unit = 8
    early = atoms + (9 + 2 * REST) * sends
    vmem = pl.BlockSpec(memory_space=pltpu.VMEM)
    smem = pl.BlockSpec(memory_space=pltpu.SMEM)
    hbm = pl.BlockSpec(memory_space=pltpu.HBM)
    copies = 26 + 26 * 1 + 19 + 8
    operands = (
        species.reshape(1, atoms), send_list.reshape(1, sends), edge_vectors.reshape(3, 1, edges),
        edge_neighbour.reshape(1, edges), edge_center.reshape(1, edges),
        embed, jnp.swapaxes(w_src, 1, 2), w_rad0, w_rad1, w_inv, w_out, jnp.swapaxes(w_gate, 1, 2),
        w_energy.reshape(1, width),
    )
    energies, forces = pl.pallas_call(
        body,
        out_shape=(
            jax.ShapeDtypeStruct((1, atoms), F32),
            jax.ShapeDtypeStruct((3, 1, atoms), F32),
        ),
        in_specs=[smem, smem] + [hbm] * len(operands),
        out_specs=(vmem, vmem),
        scratch_shapes=[pltpu.VMEM(operand.shape, operand.dtype) for operand in operands] + [
            pltpu.VMEM((atoms + ghosts, edges), BF16),
            pltpu.VMEM((atoms, edges), BF16),
            pltpu.VMEM((32, edges), BF16),
            pltpu.VMEM((atoms, edges), BF16),
            pltpu.VMEM((27 * unit, atoms), F32),
            pltpu.VMEM((ghosts, cols), BF16),
            pltpu.VMEM((cols, early), BF16),
            pltpu.VMEM((cols, ghosts + atoms - early), BF16),
            pltpu.VMEM((cols, edges), BF16),
            pltpu.VMEM((cols, edges), BF16),
            pltpu.VMEM((8, edges), F32),
            pltpu.VMEM((8, edges), F32),
            pltpu.VMEM((8, edges), F32),
            pltpu.VMEM((16, edges), F32),
            pltpu.VMEM((2 * hid, edges), F32),
            pltpu.VMEM((width + chan, edges), F32),
            pltpu.VMEM((width, edges), F32),
            pltpu.VMEM((width + chan, edges), F32),
            pltpu.VMEM((width, width), BF16),
            pltpu.VMEM((width, chan), BF16),
            pltpu.VMEM((width, chan), BF16),
            pltpu.VMEM((2, width, width), BF16),
            pltpu.VMEM((width + chan, 16), BF16),
            pltpu.VMEM((width, atoms), F32),
            pltpu.VMEM((width, width), F32),
            pltpu.VMEM((32 * unit, edges), BF16),
            pltpu.VMEM((cols, atoms), F32),
            pltpu.VMEM((width, atoms), F32),
            pltpu.VMEM((8, edges), F32),
            pltpu.VMEM((1, edges), F32),
            pltpu.VMEM((8, edges), F32),
            pltpu.VMEM((9 * sends, cols), BF16),
            pltpu.VMEM((9 * sends, cols), BF16),
            pltpu.VMEM((9 * sends, cols), BF16),
            pltpu.VMEM((9 * sends, cols), BF16),
            pltpu.VMEM((9 * sends, cols), BF16),
            pltpu.VMEM((9 * sends, cols), BF16),
            pltpu.VMEM((2, sends, cols), BF16),
            pltpu.VMEM((2, sends, cols), BF16),
            pltpu.VMEM((32 * unit, 128), F32),
            pltpu.VMEM((3, 3 * unit, 128), F32),
            pltpu.VMEM((3, 3 * unit, 128), F32),
            pltpu.VMEM((9 * unit, 128), F32),
            pltpu.VMEM((9 * unit, 128), F32),
            pltpu.VMEM((2, 3 * unit, 128), F32),
            pltpu.VMEM((2, 3 * unit, 128), F32),
            pltpu.VMEM((2, unit, 128), F32),
            pltpu.VMEM((2, unit, 128), F32),
            pltpu.SemaphoreType.DMA((copies,)),
            pltpu.SemaphoreType.DMA((copies,)),
            pltpu.SemaphoreType.DMA((len(operands),)),
        ],
        compiler_params=pltpu.CompilerParams(
            collective_id=0, has_side_effects=True, vmem_limit_bytes=56 * 1024 * 1024
        ),
    )(atom_count, edge_count, *operands)
    return energies.reshape(species.shape), forces.reshape(edge_vectors.shape[:3] + (3, atoms))


def solution(mesh):
    shard = P("gx", "gy", "gz", None)
    count = P("gx", "gy", "gz")
    wide = P("gx", "gy", "gz", None, None)
    return jax.shard_map(
        per_device,
        mesh=mesh,
        in_specs=(shard, count, shard, count, shard, shard, wide) + (P(),) * 8,
        out_specs=(shard, wide),
        check_vma=False,
    )
```

```python
import functools
import math

import jax
import jax.numpy as jnp
from jax import lax
from jax.experimental import pallas as pl
from jax.experimental.pallas import tpu as pltpu
from jax.sharding import PartitionSpec as P

RADIAL = 8
CUTOFF = 5.0
PLANE = ((1, 0), (1, 1), (1, 2), (0, 1), (2, 1), (0, 0), (0, 2), (2, 0), (2, 2))
REST = 5
OTHER, OWN, MATE = 0, 1, 2


def position(b, a, c):
    index = PLANE.index((c, a))
    if b == OWN:
        return index
    if index < REST:
        return 9 + (b // 2) * REST + index
    return 9 + 2 * REST + (b // 2) * (9 - REST) + index - REST


MESH = pl.DeviceIdType.MESH
BF16 = jnp.bfloat16
F32 = jnp.float32


def mm(left, right):
    return lax.dot_general(left, right, (((1,), (0,)), ((), ())), preferred_element_type=F32)


def mm_nt(left, right):
    return lax.dot_general(left, right, (((1,), (1,)), ((), ())), preferred_element_type=F32)


def eye(rows, cols):
    first = lax.broadcasted_iota(jnp.int32, (rows, cols), 0)
    second = lax.broadcasted_iota(jnp.int32, (rows, cols), 1)
    return jnp.where(first == second, 1.0, 0.0).astype(BF16)


def turned(array):
    return mm_nt(eye(array.shape[1], array.shape[1]), array).astype(BF16)


def split(array):
    high = array.astype(BF16).astype(F32)
    return jnp.concatenate([high, array - high], axis=0).astype(BF16)


def joined(array):
    half = array.shape[0] // 2
    return array[:half] + array[half:]


def sum_rows(array):
    return jnp.sum(array, axis=0, keepdims=True)


def sin_cos(angle):
    y = angle - (math.pi / 2)
    y2 = y * y
    sin_y = jnp.full_like(y, -1.0 / math.factorial(11))
    for power in (9, 7, 5, 3, 1):
        sin_y = sin_y * y2 + ((-1.0) ** (power // 2)) / math.factorial(power)
    cos_y = jnp.full_like(y, 1.0 / math.factorial(12))
    for power in (10, 8, 6, 4, 2, 0):
        cos_y = cos_y * y2 + ((-1.0) ** (power // 2)) / math.factorial(power)
    return cos_y, -(sin_y * y)


def body(
    atom_count, edge_count, *refs
):
    args, (energies, forces), held = refs[:13], refs[13:15], refs[15:28]
    (
        onehot, onehot_c, block_of, slot_of, kinds, halo, table, last_table, picked, dmsg,
        geo, harm, dbas, basis, slope, rad1, rad2, proj1, src2, gate_w, inv_t, out_t, kind_proj, start, readout, f_rows, agg, agg2, grad_y, grad_d, pull,
        back_send_o, back_recv_o, back_send_m, back_recv_m, back_send_x, back_recv_x, back_send_z, back_recv_z,
        f_all, f_send_o, f_recv_o, f_send_m, f_recv_m, f_send_x, f_recv_x, f_send_z, f_recv_z,
        send_sems, recv_sems, arg_sems,
    ) = refs[28:]
    (
        species, send_list, vectors, neighbour, center,
        embed, w_src, w_rad0, w_rad1, w_inv, w_out, w_gate, w_energy,
    ) = held
    atoms = species.shape[1]
    edges = center.shape[1]
    sends = send_list.shape[1]
    width = w_out.shape[1]
    chan = w_gate.shape[1]
    rows_y = 9 * sends
    rest = REST * sends
    corner = 9 * sends - rest
    early = atoms + 27 * sends - 2 * corner
    unit = 8
    blocks = atoms // sends + 27

    parity = lax.rem(lax.axis_index("gy"), 2)
    plane_by = {OTHER: 2 * parity - 1, OWN: 0, MATE: 1 - 2 * parity}

    def device(plane=OWN, **steps):
        result = {}
        if plane != OWN:
            steps["gy"] = plane_by[plane]
        for axis, by in steps.items():
            size = lax.axis_size(axis)
            result[axis] = lax.rem(lax.axis_index(axis) + size + by, size)
        return result

    loads = [
        pltpu.make_async_copy(source, target, arg_sems.at[i])
        for i, (source, target) in enumerate(zip(args, held))
    ]
    for load in loads[:2]:
        load.start()

    barrier = pltpu.get_barrier_semaphore()
    greeted = [device(gz=by) for by in (1, -1)] + [device(gx=by) for by in (1, -1)]
    greeted += [device(OTHER), device(MATE)] + [device(OTHER, gx=by) for by in (1, -1)]
    for other in greeted:
        pl.semaphore_signal(barrier, inc=1, device_id=other, device_id_type=MESH)
    for load in loads[2:5]:
        load.start()

    next_sem = [0]
    started = []

    def send(source, target, other):
        slot = next_sem[0]
        next_sem[0] = slot + 1
        copy = pltpu.make_async_remote_copy(
            src_ref=source, dst_ref=target, send_sem=send_sems.at[slot], recv_sem=recv_sems.at[slot],
            device_id=other, device_id_type=MESH,
        )
        copy.start()
        started.append(copy)
        return copy

    def settle(count):
        for copy in started[:count]:
            copy.wait_send()
        del started[:count]

    def spread(ref, size, pieces, between, straight=False):
        near, last = [], []

        def at(b, a, c, piece):
            return ref.at[pl.ds(position(b, a, c) * size + piece * (size // pieces), size // pieces)]

        def arrived(copies):
            for copy in copies:
                copy.wait_recv()

        def along(c, piece):
            copies = [send(at(OWN, 1, c, piece), at(OWN, a, c, piece), device(gx=1 - a)) for a in (0, 2)]
            for a in (0, 2) if straight else ():
                last.append(send(at(OWN, 1, c, piece), at(OTHER, a, c, piece), device(OTHER, gx=1 - a)))
            return copies

        def across(a, c, piece):
            planes = (MATE,) if straight and a != 1 else (OTHER, MATE)
            return [send(at(OWN, a, c, piece), at(b, a, c, piece), device(b)) for b in planes]

        every = range(pieces)
        in_z = [
            [send(at(OWN, 1, 1, piece), at(OWN, 1, c, piece), device(gz=1 - c)) for c in (0, 2)] for piece in every
        ]
        in_x = [along(1, piece) for piece in every]
        for piece in every:
            near += across(1, 1, piece)
        between[0]()
        for piece in every:
            arrived(in_x[piece])
            near += across(0, 1, piece) + across(2, 1, piece)
        in_x = []
        for piece in every:
            arrived(in_z[piece])
            in_x.append(along(0, piece) + along(2, piece))
            near += across(1, 0, piece) + across(1, 2, piece)
        between[1]()
        for piece in every:
            arrived(in_x[piece])
            for c in (0, 2):
                last += across(0, c, piece) + across(2, c, piece)
        arrived(near)
        between[2]()
        arrived(last)

    loads[0].wait()
    loads[1].wait()
    lane = lax.broadcasted_iota(jnp.int32, (atoms, atoms), 0)
    kind_t = jnp.where(lane == species[...], 1.0, 0.0).astype(BF16)
    lend_t = jnp.where(
        lax.broadcasted_iota(jnp.int32, (atoms, sends), 0) == send_list[...], 1.0, 0.0
    ).astype(BF16)
    species_rows = jnp.broadcast_to(species[...].astype(F32), (unit, atoms))
    own_kinds = pl.ds(position(OWN, 1, 1) * unit, unit)
    kinds[own_kinds, :] = jnp.zeros((unit, atoms), F32)
    kinds[own_kinds, pl.ds(0, sends)] = mm(species_rows.astype(BF16), lend_t)
    pl.semaphore_wait(barrier, len(greeted))


    def geometry():
        for load in loads[5:]:
            load.start()
        for load in loads[2:5]:
            load.wait()
        live = lax.broadcasted_iota(jnp.int32, (1, edges), 1) < edge_count[0, 0, 0]
        x = jnp.where(live, vectors[0], 1.0)
        y = jnp.where(live, vectors[1], 1.0)
        z = jnp.where(live, vectors[2], 1.0)
        square = x * x + y * y + z * z
        inverse = lax.rsqrt(square)
        distance = square * inverse
        ux, uy, uz = x * inverse, y * inverse, z * inverse
        for row, value in enumerate((ux, uy, uz, inverse)):
            geo[pl.ds(row, 1), :] = value
        for row, value in enumerate((
            ux, uy, uz, root * ux * uy, root * uy * uz, 0.5 * (3.0 * uz * uz - 1.0), root * ux * uz,
            0.5 * root * (ux * ux - uy * uy),
        )):
            harm[pl.ds(row, 1), :] = value
        sine, cosine = sin_cos(distance * (math.pi / CUTOFF))
        ratio = distance * (1.0 / CUTOFF)
        rest = 1.0 - ratio * ratio
        scale = rest * rest * inverse
        dscale = -(4.0 / CUTOFF) * rest * ratio * inverse - scale * inverse
        sin_k, cos_k = sine, cosine
        basis[...] = jnp.zeros_like(basis)
        for k in range(1, RADIAL + 1):
            basis[pl.ds(k - 1, 1), :] = sin_k * scale
            dbas[pl.ds(k - 1, 1), :] = (k * math.pi / CUTOFF) * cos_k * scale + sin_k * dscale
            sin_k, cos_k = sin_k * cosine + cos_k * sine, cos_k * cosine - sin_k * sine

        place = jnp.where(live, neighbour[...], -1)
        middle = jnp.where(live, center[...], -1)
        block = lax.shift_right_arithmetic(place, sends.bit_length() - 1)
        slot = lax.bitwise_and(place, sends - 1)
        planes = {plane: 1 + by for plane, by in plane_by.items()}
        order = {
            position(b, a, c): (a * 3 + planes[b]) * 3 + c for a in range(3) for b in planes for c in range(3)
        }
        rows = lax.broadcasted_iota(jnp.int32, (32, 1), 0)
        block_ids = rows
        for i in range(27):
            block_ids = jnp.where(rows == atoms // sends + i, atoms // sends + order[i], block_ids)
        block_of[...] = jnp.where(block_ids == block, 1.0, 0.0).astype(BF16)
        rows = lax.broadcasted_iota(jnp.int32, (atoms, edges), 0)
        slot_of[...] = jnp.where(rows == slot, 1.0, 0.0).astype(BF16)
        onehot_c[...] = jnp.where(rows == middle, 1.0, 0.0).astype(BF16)
        onehot[pl.ds(0, atoms), :] = jnp.where(rows == place, 1.0, 0.0).astype(BF16)
        rows = lax.broadcasted_iota(jnp.int32, (sends, edges), 0)
        for i in range(27):
            onehot[pl.ds(atoms + i * sends, sends), :] = jnp.where(
                rows == place - (atoms + order[i] * sends), 1.0, 0.0
            ).astype(BF16)

    def sweep(tile, work):
        if tile < 0:
            for i in range(edges // -tile):
                work(pl.ds(i * -tile, -tile))
        elif tile == edges:
            work(pl.ds(0, edges))
        else:
            lax.fori_loop(
                0, edges // tile, lambda i, carry: (work(pl.ds(pl.multiple_of(i * tile, tile), tile)), carry)[1], 0
            )

    def radial():
        for load in loads[5:]:
            load.wait()
        rad0_t = jnp.concatenate(
            [
                turned(
                    jnp.concatenate(
                        [w_rad0[l].astype(F32), jnp.zeros((8, w_rad0.shape[2]), F32)], axis=0
                    ).astype(BF16)
                ).astype(F32)
                for l in range(2)
            ],
            axis=0,
        ).astype(BF16)
        rad1_t1 = turned(w_rad1[0][:, : width + chan])
        rad1_t2 = turned(w_rad1[1][:, :width])

        def prepare(span):
            pre = mm(rad0_t, basis[:, span].astype(BF16))
            sig = jax.nn.sigmoid(pre)
            slope[:, span] = sig * (1.0 + pre * (1.0 - sig))
            hidden = (pre * sig).astype(BF16)
            rad1[:, span] = mm(rad1_t1, hidden[:hid])
            rad2[:, span] = mm(rad1_t2, hidden[hid:])

        sweep(edges, prepare)

        src2[...] = turned(w_src[1][:width])
        gate_w[...] = turned(w_gate[0])
        inv_t[...] = turned(w_inv[1])
        for layer in range(2):
            out_t[layer] = turned(w_out[layer])
        embed_rows = jnp.concatenate([embed[...], jnp.zeros((16 - embed.shape[0], width), F32)], axis=0)
        embed_t = turned(embed_rows.astype(BF16))
        kind_proj[...] = mm(w_src[0], embed_t).astype(BF16)
        start[...] = mm(embed_t, kind_t[:16, :])
        readout[...] = jnp.broadcast_to(w_energy[...], (width, width)).T

    root = math.sqrt(3.0)
    hid = w_rad0.shape[2]
    spread(kinds, unit, 1, (geometry, radial, lambda: None), straight=True)
    lend_wide = mm_nt(eye(128, sends), lend_t).astype(BF16)
    lend = lend_wide[:sends]

    number = species_rows[:1]
    kind_rows = [number] + [pltpu.roll(number, atoms - j * sends, 1) for j in range(1, atoms // sends)]
    kind_rows += [kinds[pl.ds(i * unit, 1), :] for i in range(27)]
    kind_rows += [jnp.zeros((1, atoms), F32)] * (32 - blocks)
    kind_table = mm_nt(eye(sends, atoms), jnp.concatenate(kind_rows, axis=0).astype(BF16)).astype(BF16)

    def layer_one(span):
        kind = sum_rows(mm(kind_table, block_of[:, span]) * slot_of[pl.ds(0, sends), span].astype(F32))
        kind_ids = lax.broadcasted_iota(jnp.int32, (16, kind.shape[1]), 0).astype(F32)
        proj = mm(kind_proj[...], jnp.where(kind_ids == kind, 1.0, 0.0).astype(BF16))
        proj1[:, span] = proj
        lead_s = proj[:width] * rad1[pl.ds(0, width), span]
        lead_t = proj[width:] * rad1[pl.ds(width, chan), span]
        parts = [lead_s.astype(BF16)]
        for m in range(8):
            parts.append((lead_t * harm[pl.ds(m, 1), span]).astype(BF16))
        agg[...] = mm_nt(jnp.concatenate(parts, axis=0), onehot_c[:, span])

    sweep(edges, layer_one)
    gathered = 0.25 * agg[...]
    gathered_t = gathered[width:]
    rounded = gathered[:width].astype(BF16)
    pre1 = mm(out_t[0], rounded)
    sig1 = jax.nn.sigmoid(pre1)
    gate = jax.nn.sigmoid(mm(w_gate[0], rounded))
    scalars = (start[...] + pre1 * sig1).astype(BF16)
    gates = jnp.concatenate([gate] * 8, axis=0)
    tensors = (gathered_t * gates).astype(BF16)
    proj2 = mm(w_src[1], scalars).astype(BF16)
    local = jnp.concatenate([proj2[:width], tensors], axis=0)
    halo[pl.ds(position(OWN, 1, 1) * sends, sends), :] = mm_nt(lend, local).astype(BF16)
    table[:, pl.ds(0, atoms)] = local
    earlier = len(started)

    def lookup(span):
        picked[:, span] = mm(table[...], onehot[pl.ds(0, early), span]).astype(BF16)

    def early_rows():
        table[:, pl.ds(atoms, early - atoms)] = halo[pl.ds(0, early - atoms), :].T
        sweep(edges, lookup)

    spread(halo, sends, 1, (lambda: settle(earlier), lambda: None, early_rows))
    last_table[...] = halo[pl.ds(early - atoms, 2 * corner), :].T

    def layer_two(span):
        rows = picked[:, span].astype(F32) + mm(last_table[...], onehot[pl.ds(early, 2 * corner), span])
        picked[:, span] = rows.astype(BF16)
        inner = jnp.zeros((chan, span.size), F32)
        for m in range(8):
            inner += rows[width + m * chan : width + (m + 1) * chan] * harm[pl.ds(m, 1), span]
        message = rows[:width] * rad2[:, span] + mm(inv_t[...], inner.astype(BF16))
        agg2[...] = mm_nt(message.astype(BF16), onehot_c[:, span])

    sweep(edges, layer_two)
    rounded = (0.25 * agg2[...]).astype(BF16)
    pre2 = mm(out_t[1], rounded)
    sig2 = jax.nn.sigmoid(pre2)
    mask = jnp.where(
        lax.broadcasted_iota(jnp.int32, (1, atoms), 1) < atom_count[0, 0, 0], 1.0, 0.0
    )
    energies[...] = mask * sum_rows((scalars.astype(F32) + pre2 * sig2) * readout[...])

    d_new = readout[...] * mask
    d_pre = (d_new * sig2 * (1.0 + pre2 * (1.0 - sig2))).astype(BF16)
    d_agg = (0.25 * mm(w_out[1], d_pre).astype(BF16).astype(F32)).astype(BF16)

    def back_two(span):
        d_msg = mm(d_agg, onehot_c[:, span])
        dmsg[pl.ds(0, width), span] = (d_msg * rad2[:, span]).astype(BF16)
        d_inv = mm(w_inv[1], d_msg.astype(BF16))
        for m in range(8):
            dmsg[pl.ds(width + m * chan, chan), span] = (d_inv * harm[pl.ds(m, 1), span]).astype(BF16)

    sweep(edges, back_two)
    earlier = len(started)

    def scattered(plane, corners):
        first = atoms + position(plane, *PLANE[REST if corners else 0][::-1]) * sends
        return mm_nt(onehot[pl.ds(first, corner if corners else rest), :], dmsg[...])

    def rows_of(c, a):
        return pl.ds(PLANE.index((c, a)) * sends, sends)

    halves = {True: pl.ds(rest, corner), False: pl.ds(0, rest)}
    back_o, back_m, back_x, plane = {}, {}, {}, {}

    def over(c, a):
        rows = rows_of(c, a)
        back_o[c, a] = send(back_send_o.at[rows], back_recv_o.at[rows], device(OTHER, gx=a - 1))

    def to_mate(corners):
        rows = halves[corners]
        back_send_m[rows] = scattered(MATE, corners).astype(BF16)
        back_m[corners] = send(back_send_m.at[rows], back_recv_m.at[rows], device(MATE))

    def own_rows(corners):
        sums = scattered(OWN, corners)
        back_m[corners].wait_recv()
        sums = sums + back_recv_m[halves[corners]].astype(F32)
        cells = PLANE[REST:] if corners else PLANE[:REST]
        for i, cell in enumerate(cells):
            plane[cell] = sums[i * sends : (i + 1) * sends]
        for c, a in cells:
            if a != 1:
                rows = rows_of(c, a)
                back_send_x[rows] = plane[c, a].astype(BF16)
                back_x[c, a] = send(back_send_x.at[rows], back_recv_x.at[rows], device(gx=a - 1))

    back_send_o[halves[True]] = scattered(OTHER, True).astype(BF16)
    for cell in PLANE[REST:]:
        over(*cell)
    to_mate(True)
    own_rows(True)
    back_send_o[halves[False]] = scattered(OTHER, False).astype(BF16)
    for cell in PLANE[:REST]:
        over(*cell)
    to_mate(False)
    own_rows(False)
    d_local = mm_nt(dmsg[...], onehot[pl.ds(0, atoms), :])

    def edge_two(span):
        d_msg = mm(d_agg, onehot_c[:, span])
        d_inv = mm(w_inv[1], d_msg.astype(BF16))
        for m in range(8):
            grad_y[pl.ds(m, 1), span] = sum_rows(
                d_inv * picked[pl.ds(width + m * chan, chan), span].astype(F32)
            )
        d_rad = (d_msg * picked[pl.ds(0, width), span].astype(F32)).astype(BF16)
        d_hid = mm(w_rad1[1][:, :width], d_rad) * slope[pl.ds(hid, hid), span]
        d_bas = mm(w_rad0[1], d_hid.astype(BF16))
        grad_d[:, span] = sum_rows(d_bas * dbas[:, span])

    sweep(edges, edge_two)

    settle(earlier)

    def gathered(c):
        total = plane[c, 1]
        for a in range(3):
            back_o[c, a].wait_recv()
            total = total + back_recv_o[rows_of(c, a)].astype(F32)
        for a in (0, 2):
            back_x[c, a].wait_recv()
            total = total + back_recv_x[rows_of(c, a)].astype(F32)
        return total

    back_z = []
    for slot, c in ((0, 0), (1, 2)):
        back_send_z[slot] = gathered(c).astype(BF16)
        back_z.append(send(back_send_z.at[slot], back_recv_z.at[slot], device(gz=c - 1)))
    back = gathered(1)
    settle(len(started) - 2)
    for copy in back_z:
        copy.wait_recv()
    back = back + back_recv_z[0].astype(F32) + back_recv_z[1].astype(F32)
    owned = d_local + mm(back.T.astype(BF16), lend)

    d_scalars = (d_new + mm(src2[...], owned[:width].astype(BF16))).astype(BF16).astype(F32)
    d_tensors = owned[width:].astype(BF16).astype(F32)
    d_pre = (d_scalars * sig1 * (1.0 + pre1 * (1.0 - sig1))).astype(BF16)
    product = d_tensors * gathered_t
    d_gate = jnp.zeros((chan, atoms), F32)
    for m in range(8):
        d_gate += product[m * chan : (m + 1) * chan]
    d_gate = (d_gate * gate * (1.0 - gate)).astype(BF16)
    d_scalar_agg = (mm(w_out[0], d_pre) + mm(gate_w[...], d_gate)).astype(BF16).astype(F32)
    d_agg1 = (0.25 * jnp.concatenate([d_scalar_agg, d_tensors * gates], axis=0)).astype(BF16)

    def edge_one(span):
        d_msg = mm(d_agg1, onehot_c[:, span])
        proj = proj1[:, span]
        lead_t = proj[width:] * rad1[pl.ds(width, chan), span]
        inner = jnp.zeros((chan, span.size), F32)
        gy = []
        for m in range(8):
            d_part = d_msg[width + m * chan : width + (m + 1) * chan]
            inner += d_part * harm[pl.ds(m, 1), span]
            gy.append(grad_y[pl.ds(m, 1), span] + sum_rows(d_part * lead_t))
        d_rad = jnp.concatenate([d_msg[:width], inner], axis=0) * proj
        d_hid = mm(w_rad1[0][:, : width + chan], d_rad.astype(BF16)) * slope[pl.ds(0, hid), span]
        d_bas = mm(w_rad0[0], d_hid.astype(BF16))
        gd = grad_d[:, span] + sum_rows(d_bas * dbas[:, span])
        ax, ay, az = geo[0:1, span], geo[1:2, span], geo[2:3, span]
        gux = gy[0] + root * (ay * gy[3] + az * gy[6] + ax * gy[7])
        guy = gy[1] + root * (ax * gy[3] + az * gy[4] - ay * gy[7])
        guz = gy[2] + root * (ay * gy[4] + ax * gy[6]) + 3.0 * az * gy[5]
        radial = gd - geo[3:4, span] * (ax * gux + ay * guy + az * guz)
        pull[pl.ds(0, 1), span] = geo[3:4, span] * gux + ax * radial
        pull[pl.ds(1, 1), span] = geo[3:4, span] * guy + ay * radial
        pull[pl.ds(2, 1), span] = geo[3:4, span] * guz + az * radial

    pull[...] = jnp.zeros_like(pull)
    sweep(edges, edge_one)

    pulls = pull[...]
    high = pulls.astype(BF16).astype(F32)
    pulls = high + pltpu.roll(pulls - high, 3, 0)
    for i in range(0, 32, 2):
        f_rows[pl.ds(i * unit, 2 * unit), :] = jnp.concatenate(
            [pulls * block_of[pl.ds(j, 1), :].astype(F32) for j in (i, i + 1)], axis=0
        ).astype(BF16)
    f_all[...] = mm_nt(f_rows[...], slot_of[...])
    first = (atoms // sends) * unit

    def cell(b, a, c):
        return f_all[pl.ds(first + position(b, a, c) * unit, unit), :]

    for a in range(3):
        f_send_o[a] = jnp.concatenate([cell(OTHER, a, c) for c in range(3)], axis=0)
    f_send_m[...] = jnp.concatenate([cell(MATE, a, c) for a in range(3) for c in range(3)], axis=0)
    f_m = send(f_send_m, f_recv_m, device(MATE))
    f_o = [send(f_send_o.at[a], f_recv_o.at[a], device(OTHER, gx=a - 1)) for a in (0, 2, 1)]
    lines = jnp.concatenate([cell(OWN, a, c) for a in range(3) for c in range(3)], axis=0)
    f_m.wait_recv()
    lines = lines + f_recv_m[...]
    f_x = []
    for slot, a in ((0, 0), (1, 2)):
        f_send_x[slot] = lines[3 * a * unit : 3 * (a + 1) * unit]
        f_x.append(send(f_send_x.at[slot], f_recv_x.at[slot], device(gx=a - 1)))
    total = mm_nt(pulls.astype(BF16), onehot_c[...])
    for j in range(atoms // sends):
        block = f_all[pl.ds(j * unit, unit), :]
        total = total - (block if j == 0 else pltpu.roll(block, j * sends, 1))
    settle(len(started) - 2)
    for copy in f_x + f_o:
        copy.wait_recv()
    lines = lines[3 * unit : 6 * unit] + f_recv_x[0] + f_recv_x[1] + f_recv_o[0] + f_recv_o[1] + f_recv_o[2]
    f_z = []
    for slot, c in ((0, 0), (1, 2)):
        f_send_z[slot] = lines[c * unit : (c + 1) * unit]
        f_z.append(send(f_send_z.at[slot], f_recv_z.at[slot], device(gz=c - 1)))
    for copy in f_z:
        copy.wait_recv()
    lines = lines[unit : 2 * unit] + f_recv_z[0] + f_recv_z[1]
    total = total - joined(mm(split(lines), lend_wide))
    for row in range(3):
        forces[row] = total[row : row + 1] + total[row + 3 : row + 4]
    settle(len(started))


def per_device(
    species, atom_count, send_list, edge_count, edge_center, edge_neighbour, edge_vectors,
    embed, w_src, w_rad0, w_rad1, w_inv, w_out, w_gate, w_energy,
):
    atoms = species.shape[-1]
    edges = edge_center.shape[-1]
    sends = send_list.shape[-1]
    width = w_out.shape[1]
    chan = w_gate.shape[2]
    hid = w_rad0.shape[2]
    cols = width + 8 * chan
    ghosts = 27 * sends
    unit = 8
    early = atoms + (9 + 2 * REST) * sends
    vmem = pl.BlockSpec(memory_space=pltpu.VMEM)
    smem = pl.BlockSpec(memory_space=pltpu.SMEM)
    hbm = pl.BlockSpec(memory_space=pltpu.HBM)
    copies = 26 + 26 * 1 + 19 + 8
    operands = (
        species.reshape(1, atoms), send_list.reshape(1, sends), edge_vectors.reshape(3, 1, edges),
        edge_neighbour.reshape(1, edges), edge_center.reshape(1, edges),
        embed, jnp.swapaxes(w_src, 1, 2), w_rad0, w_rad1, w_inv, w_out, jnp.swapaxes(w_gate, 1, 2),
        w_energy.reshape(1, width),
    )
    energies, forces = pl.pallas_call(
        body,
        out_shape=(
            jax.ShapeDtypeStruct((1, atoms), F32),
            jax.ShapeDtypeStruct((3, 1, atoms), F32),
        ),
        in_specs=[smem, smem] + [hbm] * len(operands),
        out_specs=(vmem, vmem),
        scratch_shapes=[pltpu.VMEM(operand.shape, operand.dtype) for operand in operands] + [
            pltpu.VMEM((atoms + ghosts, edges), BF16),
            pltpu.VMEM((atoms, edges), BF16),
            pltpu.VMEM((32, edges), BF16),
            pltpu.VMEM((atoms, edges), BF16),
            pltpu.VMEM((27 * unit, atoms), F32),
            pltpu.VMEM((ghosts, cols), BF16),
            pltpu.VMEM((cols, early), BF16),
            pltpu.VMEM((cols, ghosts + atoms - early), BF16),
            pltpu.VMEM((cols, edges), BF16),
            pltpu.VMEM((cols, edges), BF16),
            pltpu.VMEM((8, edges), F32),
            pltpu.VMEM((8, edges), F32),
            pltpu.VMEM((8, edges), F32),
            pltpu.VMEM((16, edges), F32),
            pltpu.VMEM((2 * hid, edges), F32),
            pltpu.VMEM((width + chan, edges), F32),
            pltpu.VMEM((width, edges), F32),
            pltpu.VMEM((width + chan, edges), F32),
            pltpu.VMEM((width, width), BF16),
            pltpu.VMEM((width, chan), BF16),
            pltpu.VMEM((width, chan), BF16),
            pltpu.VMEM((2, width, width), BF16),
            pltpu.VMEM((width + chan, 16), BF16),
            pltpu.VMEM((width, atoms), F32),
            pltpu.VMEM((width, width), F32),
            pltpu.VMEM((32 * unit, edges), BF16),
            pltpu.VMEM((cols, atoms), F32),
            pltpu.VMEM((width, atoms), F32),
            pltpu.VMEM((8, edges), F32),
            pltpu.VMEM((1, edges), F32),
            pltpu.VMEM((8, edges), F32),
            pltpu.VMEM((9 * sends, cols), BF16),
            pltpu.VMEM((9 * sends, cols), BF16),
            pltpu.VMEM((9 * sends, cols), BF16),
            pltpu.VMEM((9 * sends, cols), BF16),
            pltpu.VMEM((9 * sends, cols), BF16),
            pltpu.VMEM((9 * sends, cols), BF16),
            pltpu.VMEM((2, sends, cols), BF16),
            pltpu.VMEM((2, sends, cols), BF16),
            pltpu.VMEM((32 * unit, 128), F32),
            pltpu.VMEM((3, 3 * unit, 128), F32),
            pltpu.VMEM((3, 3 * unit, 128), F32),
            pltpu.VMEM((9 * unit, 128), F32),
            pltpu.VMEM((9 * unit, 128), F32),
            pltpu.VMEM((2, 3 * unit, 128), F32),
            pltpu.VMEM((2, 3 * unit, 128), F32),
            pltpu.VMEM((2, unit, 128), F32),
            pltpu.VMEM((2, unit, 128), F32),
            pltpu.SemaphoreType.DMA((copies,)),
            pltpu.SemaphoreType.DMA((copies,)),
            pltpu.SemaphoreType.DMA((len(operands),)),
        ],
        compiler_params=pltpu.CompilerParams(
            collective_id=0, has_side_effects=True, vmem_limit_bytes=56 * 1024 * 1024
        ),
    )(atom_count, edge_count, *operands)
    return energies.reshape(species.shape), forces.reshape(edge_vectors.shape[:3] + (3, atoms))


def solution(mesh):
    shard = P("gx", "gy", "gz", None)
    count = P("gx", "gy", "gz")
    wide = P("gx", "gy", "gz", None, None)
    return jax.shard_map(
        per_device,
        mesh=mesh,
        in_specs=(shard, count, shard, count, shard, shard, wide) + (P(),) * 8,
        out_specs=(shard, wide),
        check_vma=False,
    )
```
